512 devices in a mesh: pm: 2 (over y_lo), ka: 128 (over x, z, core), isdf: 2 (over y_hi).
Axes of the slice: x: 4, y: 4 (y_hi: 2, y_lo: 2; y = y_hi * 2 + y_lo), z: 16, core: 2. Of those that a mesh axis runs over, the one named last changes fastest.
Arguments:
- amplitudes: bfloat16 [2, 2, 2, 256, 64, 256], P('pm', None, None, 'ka'), may hold values from -6 to 6
- conduction: bfloat16 [2, 256, 256, 512], P(None, 'ka', None, 'isdf'), may hold values from -0.375 to 0.375
- valence: bfloat16 [2, 256, 64, 512], P(None, 'ka'), may hold values from -0.75 to 0.75
- energy: float32 [256, 64, 256], P('ka', None, 'isdf'), may hold values from 0.5 to 2.5
- screened: bfloat16 [4, 2, 512, 512], P(None, None, 'isdf'), may hold values from -0.59765625 to 0.59765625
- coulomb: float32 [512, 512], P(None, 'isdf'), may hold values from -0.03125 to 0.03125
- mirror: int32 [256], P('ka'), may hold values from 0 to 255, as said below
- transfer_class: int32 [256, 256], P('ka'), may hold values from 0 to 3, as said below
Outputs:
- response: bfloat16 [2, 2, 2, 256, 64, 256], P('pm', None, None, 'ka', None, 'isdf')
The draws below stay inside these ranges and needn't reach their ends.
Inputs may be any that keep to these rules, and one draw needn't show every extreme that they name: mirror[mirror[k]] = k; a k-point of block j (the aligned block of 2 k-points that holds it) has its mirror in block 127 - j. transfer_class[k, k2] depends only on (k - k2) mod 256.
All inputs are finite; a program needn't handle non-finite values.
Results may differ from the reference program's by a relative error of at most 0.015.
Values may be sent and summed in bfloat16 or wider, within the bound.
A program may use at most 128 MiB of HBM per device.

```python
import jax
import jax.numpy as jnp
from jax import lax

NV = 64
NC = 256
NISDF = 512
VECS = 2
KDEV = 2
WBLOCKS = 4
REACH = 2
NBLK = 128
NK = 256


def draw_mirror(key, part):
    block_count = NK // KDEV
    block_keys = jax.random.split(jax.random.fold_in(key, 5), block_count)
    orderings = jax.vmap(lambda subkey: jax.random.permutation(subkey, KDEV))(block_keys).astype(jnp.int32)
    inverses = jnp.argsort(orderings, axis=1, stable=True).astype(jnp.int32)
    blocks = jnp.arange(block_count, dtype=jnp.int32)
    opposite = (block_count - 1 - blocks).astype(jnp.int32)
    nearer = jnp.minimum(blocks, opposite).astype(jnp.int32)
    forward = jnp.take(orderings, nearer, axis=0)
    backward = jnp.take(inverses, nearer, axis=0)
    within = jnp.where((blocks < opposite)[:, None], forward, backward)
    return (opposite[:, None] * KDEV + within).reshape(NK).astype(jnp.int32)


def draw_transfer_class(key, part):
    class_key, order_key = jax.random.split(jax.random.fold_in(key, 17))
    classes = jax.random.randint(class_key, (NK,), 0, WBLOCKS, dtype=jnp.int32)
    classes = classes.at[:WBLOCKS].set(jax.random.permutation(order_key, WBLOCKS).astype(jnp.int32))
    points = jnp.arange(NK, dtype=jnp.int32)
    differ = jnp.mod(points[:, None] - points[None, :], NK)
    return jnp.take(classes, differ, axis=0).astype(jnp.int32)


def level_of(stream_key, dims, pieces, low, high):
    factor_of, own = 1.0, jax.random.fold_in(stream_key, 6)
    for dim, shards_of in pieces:
        heights = jnp.exp(jax.random.uniform(jax.random.fold_in(own, dim), (shards_of,), jnp.float32, low / len(pieces), high / len(pieces)))
        factor_of = factor_of * jnp.repeat(heights, dims[dim] // shards_of).reshape([-1 if axis == dim else 1 for axis in range(len(dims))])
    return factor_of


def centred(key, extent, deviation, bound, shards=(), kind=jnp.bfloat16):
    gain = level_of(key, extent, shards, -0.22, 0.18) if shards else 1.0
    values = jax.random.normal(key, extent, jnp.float32) * deviation * gain
    return jnp.minimum(jnp.maximum(values, -bound), bound).astype(kind)


def setup_inputs(seed: int = 0) -> dict:
    streams_of = jax.random.split(jax.random.key(seed), 9)
    return {
        "amplitudes": centred(streams_of[0], (2, VECS, 2, NK, NV, NC), 1.0, 6.0, ((0, 2), (3, 128))),
        "conduction": centred(streams_of[1], (2, NK, NC, NISDF), NC ** -0.5, 0.375, ((1, 128), (3, 2))),
        "valence": centred(streams_of[2], (2, NK, NV, NISDF), NV ** -0.5, 0.75, ((1, 128),)),
        "energy": jnp.clip(0.5 + 2.0 * jax.random.uniform(streams_of[3], (NK, NV, NC), jnp.float32) ** level_of(streams_of[3], (NK, NV, NC), ((0, 128), (2, 2)), -0.2, 0.2), 0.5, 2.5),
        "screened": centred(streams_of[4], (WBLOCKS, 2, NISDF, NISDF), 0.1, 0.59765625, ((2, 2),)),
        "coulomb": centred(streams_of[5], (NISDF, NISDF), (NISDF * NK // 4) ** -0.5, 0.03125, ((1, 2),), jnp.float32),
        "mirror": draw_mirror(jax.random.fold_in(streams_of[8], 71), 0),
        "transfer_class": draw_transfer_class(jax.random.fold_in(streams_of[8], 71), 0),
    }


HIGHEST = lax.Precision.HIGHEST


def pair_einsum(pattern, left, right, conjugate):
    def single(first, second):
        return jnp.einsum(pattern, first.astype(jnp.float32), second.astype(jnp.float32), precision=HIGHEST)

    if conjugate:
        real_part = single(left[0], right[0]) + single(left[1], right[1])
        imag_part = single(left[1], right[0]) - single(left[0], right[1])
    else:
        real_part = single(left[0], right[0]) - single(left[1], right[1])
        imag_part = single(left[0], right[1]) + single(left[1], right[0])
    return real_part, imag_part


def conjugated(field):
    return jnp.stack([field[:, 0], -field[:, 1]], axis=1)


def channel(vector, conduction, valence, energy, screened, coulomb, transfer_class, weight):
    coef_real, coef_imag = pair_einsum("bkvc,kcm->bkvm", (vector[:, 0], vector[:, 1]), (conduction[0], conduction[1]), False)
    coef_real = coef_real.astype(jnp.bfloat16)
    coef_imag = coef_imag.astype(jnp.bfloat16)
    valence_real = valence[0].astype(jnp.float32)[None]
    valence_imag = valence[1].astype(jnp.float32)[None]
    coef_real_wide = coef_real.astype(jnp.float32)
    coef_imag_wide = coef_imag.astype(jnp.float32)
    rho_real = jnp.sum(valence_real * coef_real_wide + valence_imag * coef_imag_wide, axis=(1, 2))
    rho_imag = jnp.sum(valence_real * coef_imag_wide - valence_imag * coef_real_wide, axis=(1, 2))
    density = jnp.stack([rho_real, rho_imag], axis=1)
    potential = jnp.einsum("mn,brn->brm", coulomb, density, precision=HIGHEST)

    coef_by_point = jnp.moveaxis(jnp.stack([coef_real, coef_imag], axis=2), 1, 0)
    valence_by_point = jnp.moveaxis(valence, 1, 0)

    def pair_matrix(operands):
        coef_one, valence_one = operands
        real_part, imag_part = pair_einsum("bvm,vn->bmn", (coef_one[:, 0], coef_one[:, 1]), (valence_one[0], valence_one[1]), True)
        return jnp.stack([real_part, imag_part], axis=1).astype(jnp.bfloat16)

    matrices = lax.map(pair_matrix, (coef_by_point, valence_by_point))

    def block_product(block_id):
        first_point = (block_id * KDEV).astype(jnp.int32)
        total_real = jnp.zeros((VECS, KDEV, NISDF, NISDF), jnp.float32)
        total_imag = jnp.zeros((VECS, KDEV, NISDF, NISDF), jnp.float32)
        for offset in range(-REACH, REACH + 1):
            source = ((block_id + offset) % NBLK).astype(jnp.int32)
            source_point = (source * KDEV).astype(jnp.int32)
            visiting = lax.dynamic_slice_in_dim(matrices, source_point, KDEV, 0).astype(jnp.float32)
            classes = lax.dynamic_slice(transfer_class, (first_point, source_point), (KDEV, KDEV))
            chosen = jnp.take(screened, classes, axis=0).astype(jnp.float32)
            screen_real = chosen[:, :, 0][None]
            screen_imag = chosen[:, :, 1][None]
            pair_real = jnp.moveaxis(visiting[:, :, 0], 0, 1)[:, None]
            pair_imag = jnp.moveaxis(visiting[:, :, 1], 0, 1)[:, None]
            total_real = total_real + jnp.sum(screen_real * pair_real - screen_imag * pair_imag, axis=2)
            total_imag = total_imag + jnp.sum(screen_real * pair_imag + screen_imag * pair_real, axis=2)
        sum_real = total_real.astype(jnp.bfloat16)
        sum_imag = total_imag.astype(jnp.bfloat16)
        valence_block = lax.dynamic_slice_in_dim(valence, first_point, KDEV, 1)
        back_real, back_imag = pair_einsum("bkmn,kvn->bkvm", (sum_real, sum_imag), (valence_block[0], valence_block[1]), False)
        potential_real = potential[:, 0][:, None, None, :]
        potential_imag = potential[:, 1][:, None, None, :]
        block_real = valence_block[0].astype(jnp.float32)[None]
        block_imag = valence_block[1].astype(jnp.float32)[None]
        exchange_real = potential_real * block_real - potential_imag * block_imag
        exchange_imag = potential_real * block_imag + potential_imag * block_real
        field_real = (weight * exchange_real - back_real).astype(jnp.bfloat16)
        field_imag = (weight * exchange_imag - back_imag).astype(jnp.bfloat16)
        conduction_block = lax.dynamic_slice_in_dim(conduction, first_point, KDEV, 1)
        out_real, out_imag = pair_einsum("bkvm,kcm->bkvc", (field_real, field_imag), (conduction_block[0], conduction_block[1]), True)
        vector_block = lax.dynamic_slice_in_dim(vector, first_point, KDEV, 2).astype(jnp.float32)
        energy_block = lax.dynamic_slice_in_dim(energy, first_point, KDEV, 0)
        result = energy_block[None, None] * vector_block + jnp.stack([out_real, out_imag], axis=1)
        return result.astype(jnp.bfloat16)

    blocks = lax.map(block_product, jnp.arange(NBLK, dtype=jnp.int32))
    return jnp.moveaxis(blocks, 0, 2).reshape(VECS, 2, NK, NV, NC)


def reference(amplitudes, conduction, valence, energy, screened, coulomb, mirror, transfer_class):
    direct = amplitudes[0].astype(jnp.float32)
    flipped = conjugated(jnp.take(amplitudes[1], mirror, axis=2).astype(jnp.float32))
    plus_vector = (direct + flipped).astype(jnp.bfloat16)
    minus_vector = (direct - flipped).astype(jnp.bfloat16)
    plus_out = channel(plus_vector, conduction, valence, energy, screened, coulomb, transfer_class, 4.0).astype(jnp.float32)
    minus_out = channel(minus_vector, conduction, valence, energy, screened, coulomb, transfer_class, 0.0).astype(jnp.float32)
    first_half = (0.5 * (plus_out + minus_out)).astype(jnp.bfloat16)
    second_half = conjugated(jnp.take(0.5 * (plus_out - minus_out), mirror, axis=2)).astype(jnp.bfloat16)
    return jnp.stack([first_half, second_half], axis=0)
```

```python
import jax
import jax.numpy as jnp
from jax import lax
from jax.sharding import PartitionSpec as P

REACH = 2


HIGHEST = lax.Precision.HIGHEST


def swapped(block, axis, apart):
    count = lax.axis_size(axis)
    route = []
    for low in range(count):
        high = low | 1 << apart
        if high != low and high < count:
            route += [(low, high), (high, low)]
    return lax.ppermute(block, axis, route)


def shifted(value, axis, by):
    size = lax.axis_size(axis)
    return lax.ppermute(value, axis, [(i, (i + by) % size) for i in range(size)])


def pair_einsum(pattern, left, right, conjugate):

    def single(first, second):
        return jnp.einsum(pattern, first, second, preferred_element_type=jnp.float32)

    if conjugate:
        real_part = single(left[0], right[0]) + single(left[1], right[1])
        imag_part = single(left[1], right[0]) - single(left[0], right[1])
    else:
        real_part = single(left[0], right[0]) - single(left[1], right[1])
        imag_part = single(left[0], right[1]) + single(left[1], right[0])
    return (real_part, imag_part)


def conjugated(field):
    return jnp.stack([field[:, 0], -field[:, 1]], axis=1)


def coefficients(vector, conduction):
    real_part, imag_part = pair_einsum(
        "bkvc,kcm->bkvm", (vector[:, 0], vector[:, 1]), (conduction[0], conduction[1]), False
    )
    return jnp.stack([real_part, imag_part], axis=1).astype(jnp.bfloat16)


def amp_bits(field):
    for bit_number in range(lax.axis_size("ka").bit_length() - 1):
        field = swapped(field, "ka", bit_number)
    return field


def result_bits(field):
    for bit_number in range(lax.axis_size("ka").bit_length() - 1):
        field = swapped(field, "ka", bit_number)
    return field


def by_mirror(field, local_mirror):
    index = local_mirror[None, None, :, None, None]
    return jnp.where(index == 0, field[:, :, 0:1], field[:, :, 1:2])


def per_device(amplitudes, conduction, valence, energy, screened, coulomb, mirror, transfer_class):
    pm_index = lax.axis_index("pm")
    ka_index = lax.axis_index("ka")
    isdf_index = lax.axis_index("isdf")
    ka_count = lax.axis_size("ka")
    kpoint_count = conduction.shape[1]
    mu_count = conduction.shape[3]
    point_count = valence.shape[3]
    cond_share = energy.shape[2]
    vector_count = amplitudes.shape[1]
    is_plus = pm_index == 0
    parity = jnp.where(is_plus, 1.0, -1.0).astype(jnp.float32)
    exchange_weight = jnp.where(is_plus, 4.0, 0.0).astype(jnp.float32)
    local_amps = amplitudes[0]
    partner_amps = swapped(local_amps, "pm", 0)
    partner_side = jnp.where(is_plus, partner_amps, local_amps)
    distant_side = amp_bits(partner_side)
    direct = jnp.where(is_plus, local_amps, partner_amps).astype(jnp.float32)
    local_mirror = mirror - (ka_count - 1 - ka_index) * kpoint_count
    flipped = conjugated(by_mirror(distant_side, local_mirror).astype(jnp.float32))
    vector = (direct + parity * flipped).astype(jnp.bfloat16)
    own_coef = coefficients(vector, conduction)
    valence_part = lax.dynamic_slice_in_dim(valence, isdf_index * mu_count, mu_count, 3)
    rho_real = jnp.einsum(
        "kvm,bkvm->bm", valence_part[0], own_coef[:, 0], preferred_element_type=jnp.float32
    )
    rho_real = rho_real + jnp.einsum(
        "kvm,bkvm->bm", valence_part[1], own_coef[:, 1], preferred_element_type=jnp.float32
    )
    rho_imag = jnp.einsum(
        "kvm,bkvm->bm", valence_part[0], own_coef[:, 1], preferred_element_type=jnp.float32
    )
    rho_imag = rho_imag - jnp.einsum(
        "kvm,bkvm->bm", valence_part[1], own_coef[:, 0], preferred_element_type=jnp.float32
    )
    density = jnp.stack([rho_real, rho_imag], axis=1)
    spread = jnp.einsum("nm,brm->brn", coulomb, density, precision=HIGHEST)
    spread = lax.psum(spread, ("ka", "isdf"))
    potential = lax.dynamic_slice_in_dim(spread, isdf_index * mu_count, mu_count, 2)
    class_ids = jnp.arange(screened.shape[0], dtype=jnp.int32)

    def accumulate(totals, coef_block, valence_block, source):
        pair_real, pair_imag = pair_einsum(
            "bqvm,qvn->bqmn",
            (coef_block[:, 0], coef_block[:, 1]),
            (valence_block[0], valence_block[1]),
            True,
        )
        pair_real = pair_real.astype(jnp.bfloat16)
        pair_imag = pair_imag.astype(jnp.bfloat16)
        classes = lax.dynamic_slice_in_dim(transfer_class, source * kpoint_count, kpoint_count, 1)
        selector = (classes[:, :, None] == class_ids).astype(jnp.bfloat16)
        total_real, total_imag = totals
        for visitor in range(kpoint_count):
            chosen = jnp.einsum(
                "kw,wrmn->rkmn", selector[:, visitor], screened, preferred_element_type=jnp.float32
            ).astype(jnp.bfloat16)
            screen_real = chosen[0][None].astype(jnp.float32)
            screen_imag = chosen[1][None].astype(jnp.float32)
            visit_real = pair_real[:, visitor][:, None].astype(jnp.float32)
            visit_imag = pair_imag[:, visitor][:, None].astype(jnp.float32)
            total_real = total_real + (screen_real * visit_real - screen_imag * visit_imag)
            total_imag = total_imag + (screen_real * visit_imag + screen_imag * visit_real)
        return (total_real, total_imag)

    payload = (vector, conduction, valence)

    def advance(moving, offset):
        return shifted((moving[0], moving[1], moving[2]), "ka", offset)

    def unpack(moving):
        return (coefficients(moving[0], moving[1]), moving[2])

    def visit(totals, moving, distance):
        coef_block, valence_block = unpack(moving)
        source = jnp.mod(ka_index + distance, ka_count)
        return accumulate(totals, coef_block, valence_block, source)

    zero_field = jnp.zeros((vector_count, kpoint_count, mu_count, point_count), jnp.float32)
    totals = accumulate((zero_field, zero_field), own_coef, valence, ka_index)
    below_item = payload
    for count_done in range(REACH):
        below_item = advance(below_item, 1)
        totals = visit(totals, below_item, -(count_done + 1))
    above_item = payload
    for count_done in range(REACH):
        above_item = advance(above_item, -1)
        totals = visit(totals, above_item, count_done + 1)
    sum_real = totals[0].astype(jnp.bfloat16)
    sum_imag = totals[1].astype(jnp.bfloat16)
    back_real, back_imag = pair_einsum(
        "bkmn,kvn->bkvm", (sum_real, sum_imag), (valence[0], valence[1]), False
    )
    potential_real = potential[:, 0][:, None, None, :]
    potential_imag = potential[:, 1][:, None, None, :]
    exchange_real = potential_real * valence_part[0] - potential_imag * valence_part[1]
    exchange_imag = potential_real * valence_part[1] + potential_imag * valence_part[0]
    field_real = (exchange_weight * exchange_real - back_real).astype(jnp.bfloat16)
    field_imag = (exchange_weight * exchange_imag - back_imag).astype(jnp.bfloat16)
    out_real, out_imag = pair_einsum(
        "bkvm,kcm->bkvc", (field_real, field_imag), (conduction[0], conduction[1]), True
    )
    partial_out = jnp.stack([out_real, out_imag], axis=1)
    summed = lax.psum_scatter(
        partial_out.astype(jnp.bfloat16), "isdf", scatter_dimension=4, tiled=True
    ).astype(jnp.float32)
    vector_part = lax.dynamic_slice_in_dim(vector, isdf_index * cond_share, cond_share, 4).astype(
        jnp.float32
    )
    channel_out = (energy[None, None] * vector_part + summed).astype(jnp.bfloat16)
    partner_out = swapped(channel_out, "pm", 0)
    blended = (
        0.5 * (partner_out.astype(jnp.float32) + parity * channel_out.astype(jnp.float32))
    ).astype(jnp.bfloat16)
    distant_out = result_bits(blended)
    reflected = conjugated(by_mirror(distant_out, local_mirror))
    result = jnp.where(is_plus, blended, reflected)
    return result[None]


def solution(mesh):
    return jax.shard_map(
        per_device,
        mesh=mesh,
        in_specs=(
            P("pm", None, None, "ka", None, None),
            P(None, "ka", None, "isdf"),
            P(None, "ka", None, None),
            P("ka", None, "isdf"),
            P(None, None, "isdf", None),
            P(None, "isdf"),
            P("ka"),
            P("ka", None),
        ),
        out_specs=P("pm", None, None, "ka", None, "isdf"),
        check_vma=False,
    )
```

```python
import functools

import jax
import jax.numpy as jnp
from jax import lax
from jax.experimental import pallas as pl
from jax.experimental.pallas import tpu as pltpu
from jax.sharding import PartitionSpec as P

REACH = 2
KDEV = 2
SLOTS = 2 * REACH + 1
BF16 = jnp.bfloat16
F32 = jnp.float32
MESH = pl.DeviceIdType.MESH


def dot_nn(left, right):
    return lax.dot_general(left, right, (((1,), (0,)), ((), ())), preferred_element_type=F32)


def dot_nt(left, right, precision=None):
    return lax.dot_general(
        left, right, (((1,), (1,)), ((), ())), preferred_element_type=F32, precision=precision
    )


def kernel(
    grid,
    amps,
    cond_hbm,
    val_hbm,
    energy_hbm,
    screened_hbm,
    coulomb_hbm,
    mirror,
    classes,
    out,
    cond,
    vals,
    energy,
    screened,
    coulomb,
    xbuf,
    ybuf,
    gbuf,
    mbuf,
    sbuf,
    backs,
    fields,
    owns,
    rs_send,
    rs_recv,
    results,
    land_x,
    land_y,
    ar_a,
    ar_b,
    ar_c,
    rho_rows,
    u_send,
    u_recv,
    local_sem,
    send_sem,
    recv_sem,
):
    nx, nz_hi, nz_lo, nk = grid
    nz = nz_hi * nz_lo
    blocks = nx * nz * 2
    pm = lax.axis_index("pm")
    ka = lax.axis_index("ka")
    side = lax.axis_index("isdf")
    core = ka % 2
    z = (ka // 2) % nz
    x = ka // (2 * nz)
    z_lo, z_hi = z % nz_lo, z // nz_lo
    nv, nc = xbuf.shape[2], xbuf.shape[3]
    nmu = cond.shape[3]
    nnu = vals.shape[4]
    half = nc // 2

    mate = ka + 1 - 2 * core
    above = (ka + REACH) % blocks
    below = (ka + blocks - REACH) % blocks
    across = blocks - 1 - ka

    def ka_of(x_at, z_at, core_at):
        return (x_at * nz + z_at) * 2 + core_at

    a_size = 2 * nx
    a_index = x * 2 + core

    def a_peer(step):
        other = (a_index + step) % a_size
        return ka_of(other // 2, z, other % 2)

    def b_peer(step):
        return ka_of(x, z_hi * nz_lo + (z_lo + step) % nz_lo, core)

    def c_peer(step):
        return ka_of(x, ((z_hi + step) % nz_hi) * nz_lo + z_lo, core)

    here = {"pm": pm, "ka": ka, "isdf": side}

    def device(**change):
        return {**here, **change}

    counter = {"local": 0, "send": 0, "recv": 0}

    def take(kind, count=1):
        first = counter[kind]
        counter[kind] += count
        return first

    def local(src, dst):
        return pltpu.make_async_copy(src, dst, local_sem.at[take("local")])

    pending = []

    def remote(src, dst, recv, target):
        copy = pltpu.make_async_remote_copy(
            src_ref=src,
            dst_ref=dst,
            send_sem=send_sem.at[take("send")],
            recv_sem=recv_sem.at[recv],
            device_id=target,
            device_id_type=MESH,
        )
        return copy

    def launch(src, dst, recv, target):
        copy = remote(src, dst, recv, target)
        copy.start()
        pending.append(copy)

    def arrive(dst, recv):
        pltpu.make_async_remote_copy(
            src_ref=dst,
            dst_ref=dst,
            send_sem=send_sem.at[0],
            recv_sem=recv_sem.at[recv],
            device_id=device(isdf=1 - side),
            device_id_type=MESH,
        ).wait_recv()

    greeted = [
        device(pm=1 - pm),
        device(pm=0, ka=across),
        device(pm=1, ka=across),
        device(isdf=1 - side),
        device(ka=above),
        device(ka=below),
        device(ka=mate),
    ]
    greeted += [device(ka=a_peer(step)) for step in range(1, a_size)]
    greeted += [device(ka=b_peer(step)) for step in range(1, nz_lo)]
    greeted += [device(ka=c_peer(step)) for step in range(1, nz_hi)]
    barrier = pltpu.get_barrier_semaphore()
    for target in greeted:
        pl.semaphore_signal(barrier, inc=1, device_id=target, device_id_type=MESH)

    load_v = local(val_hbm, vals.at[REACH])
    load_c = local(cond_hbm, cond)
    load_x = local(amps.at[0, 0], xbuf)
    load_s = local(screened_hbm, screened)
    load_k = local(coulomb_hbm, coulomb)
    load_e = local(energy_hbm, energy)
    load_v.start()
    load_c.start()

    @pl.when(pm == 0)
    def _():
        load_x.start()

    load_s.start()
    load_k.start()
    load_e.start()
    pl.semaphore_wait(barrier, len(greeted))

    x_recv = take("recv")
    y_recv = take("recv")
    y_pass_recv = take("recv")
    v_recv = take("recv", SLOTS)
    g_recv = [take("recv", SLOTS) for _ in range(2)]
    send_x = remote(amps.at[0, 1], xbuf, x_recv, device(pm=1))
    send_y = [
        remote(amps.at[0, b, :, side], ybuf.at[:, side], y_recv, device(pm=b, ka=across)) for b in (1, 0)
    ]

    @pl.when(pm == 1)
    def _():
        for copy in send_y:
            copy.start()

    @pl.when(pm == 0)
    def _():
        send_x.start()

    mate_there = 1 + 2 * core
    mate_here = 3 - 2 * core
    pass_from = 4 - 4 * core
    pass_there = 3 - 2 * core
    passed_here = 1 + 2 * core
    direct_here = 4 * core

    def spread_block(block, landing, recv):
        launch(block, landing.at[0], recv, device(ka=above))
        launch(block, landing.at[SLOTS - 1], recv + SLOTS - 1, device(ka=below))
        launch(block, landing.at[mate_there], recv + mate_there, device(ka=mate))

    def pass_block(landing, recv):
        arrive(landing.at[pass_from], recv + pass_from)
        launch(landing.at[pass_from], landing.at[pass_there], recv + pass_there, device(ka=mate))

    spread_block(val_hbm, vals, v_recv)

    my_mu = pl.ds(pl.multiple_of(side * nmu, nmu), nmu)
    my_half = pl.ds(pl.multiple_of(side * half, half), half)

    def transform(channel, k, z_real, z_imag, sign):
        stack = jnp.concatenate([z_real, z_imag], axis=0)
        with_real = dot_nn(stack, cond[0, k])
        with_imag = dot_nn(stack, cond[1, k])
        g_real = with_real[:nv] - sign * with_imag[nv:]
        g_imag = with_imag[:nv] + sign * with_real[nv:]
        g_all = jnp.concatenate([g_real, g_imag], axis=0)
        gbuf[channel, REACH, k] = jnp.transpose(g_all).astype(BF16)
        v_real = vals[REACH, 0, k, :, my_mu].astype(F32)
        v_imag = vals[REACH, 1, k, :, my_mu].astype(F32)
        rho_real = jnp.sum(v_real * g_real + v_imag * g_imag, axis=0, keepdims=True)
        rho_imag = jnp.sum(v_real * g_imag - v_imag * g_real, axis=0, keepdims=True)
        return rho_real, rho_imag

    load_c.wait()
    load_v.wait()

    @pl.when(pm == 0)
    def _():
        load_x.wait()

    @pl.when(pm == 1)
    def _():
        arrive(xbuf, x_recv)

    rho_x = [transform(0, k, xbuf[0, k], xbuf[1, k], 1.0) for k in range(KDEV)]
    spread_block(gbuf.at[0, REACH], gbuf.at[0], g_recv[0])

    arrive(ybuf.at[:, side], y_recv)
    launch(ybuf.at[:, side], ybuf.at[:, side], y_pass_recv, device(isdf=1 - side))
    arrive(ybuf.at[:, 1 - side], y_pass_recv)
    mirrored = [lax.rem(mirror[k], KDEV) for k in range(KDEV)]
    rho_y = [transform(1, k, ybuf[0, mirrored[k]], ybuf[1, mirrored[k]], -1.0) for k in range(KDEV)]
    spread_block(gbuf.at[1, REACH], gbuf.at[1], g_recv[1])

    rho_real = sum(part[0] for part in rho_x + rho_y)
    rho_imag = sum(part[1] for part in rho_x + rho_y)
    lanes = 128
    pieces = nmu // lanes

    def put_rho(buffer, index, value):
        buffer[pl.ds(index, 1)] = value[None]

    rho_rows[...] = jnp.zeros_like(rho_rows)
    for piece in range(pieces):
        rho_rows[pl.ds(piece, 1), :] = rho_real[:, piece * lanes : (piece + 1) * lanes]
        rho_rows[pl.ds(pieces + piece, 1), :] = rho_imag[:, piece * lanes : (piece + 1) * lanes]

    def stage(buffer, index, size, peer, value):
        base = take("recv", size)
        put_rho(buffer, index, value)
        for step in range(1, size):
            launch(buffer.at[index], buffer.at[index], base + index, device(ka=peer(step)))
        return base

    def finish(buffer, index, size, base):
        for step in range(1, size):
            other = (index + step) % size
            arrive(buffer.at[other], base + other)
        return jnp.sum(buffer[...], axis=0)

    base_a = stage(ar_a, a_index, a_size, a_peer, rho_rows[...])

    def pairs(channel, slot):
        def one(k, carry):
            v_real = vals[slot, 0, k]
            v_imag = vals[slot, 1, k]
            coef = gbuf[channel, slot, k]
            at = slot * KDEV + k
            mbuf[at, 0] = dot_nn(coef, jnp.concatenate([v_real, v_imag], axis=0)).astype(BF16)
            mbuf[at, 1] = dot_nn(coef, jnp.concatenate([-v_imag, v_real], axis=0)).astype(BF16)
            return carry

        lax.fori_loop(0, KDEV, one, 0)

    shifts = SLOTS * KDEV + 1
    kinds = [classes[0, (ka * KDEV + nk - (e - SLOTS)) % nk] for e in range(shifts)]

    def screen():
        rows = 16

        def one(i, carry):
            row = pl.ds(pl.multiple_of(i * rows, rows), rows)
            for column in range(0, nnu, 128):
                col = pl.ds(column, 128)
                total = [[None, None] for _ in range(KDEV)]
                weights = [None] * shifts
                for e in range(shifts):
                    weights[e] = (screened[kinds[e], 0, row, col], screened[kinds[e], 1, row, col])
                for t in range(SLOTS * KDEV):
                    m_real = mbuf[t, 0, row, col]
                    m_imag = mbuf[t, 1, row, col]
                    for k in range(KDEV):
                        w_real, w_imag = weights[SLOTS * KDEV - 1 + k - t]
                        real = w_real * m_real - w_imag * m_imag
                        imag = w_real * m_imag + w_imag * m_real
                        old = total[k]
                        total[k] = [real, imag] if old[0] is None else [old[0] + real, old[1] + imag]
                for k in range(KDEV):
                    sbuf[k, 0, row, col] = total[k][0]
                    sbuf[k, 1, row, col] = total[k][1]
            return carry

        lax.fori_loop(0, nmu // rows, one, 0)

    def back(channel):
        for k in range(KDEV):
            stack = jnp.concatenate([vals[REACH, 0, k], vals[REACH, 1, k]], axis=0)
            with_real = dot_nt(stack, sbuf[k, 0])
            with_imag = dot_nt(stack, sbuf[k, 1])
            backs[channel, k, 0] = with_real[:nv] - with_imag[nv:]
            backs[channel, k, 1] = with_real[nv:] + with_imag[:nv]

    pairs(0, REACH)
    pass_block(vals, v_recv)
    pass_block(gbuf.at[0], g_recv[0])

    def wait_slot(landing, recv, slot):
        arrive(landing.at[slot], recv + slot)

    load_s.wait()
    for slot in (mate_here, pass_from, direct_here, passed_here):
        if slot is not pass_from:
            wait_slot(vals, v_recv, slot)
            wait_slot(gbuf.at[0], g_recv[0], slot)
        pairs(0, slot)
    base_b = stage(ar_b, z_lo, nz_lo, b_peer, finish(ar_a, a_index, a_size, base_a))
    screen()
    pass_block(gbuf.at[1], g_recv[1])
    base_c = stage(ar_c, z_hi, nz_hi, c_peer, finish(ar_b, z_lo, nz_lo, base_b))
    back(0)

    pairs(1, REACH)
    for slot in (mate_here, pass_from, direct_here, passed_here):
        if slot is not pass_from:
            wait_slot(gbuf.at[1], g_recv[1], slot)
        pairs(1, slot)

    rho = finish(ar_c, z_hi, nz_hi, base_c)
    load_k.wait()
    density = jnp.concatenate(
        [
            jnp.concatenate([rho[piece : piece + 1] for piece in range(pieces)], axis=1),
            jnp.concatenate([rho[pieces + piece : pieces + piece + 1] for piece in range(pieces)], axis=1),
            jnp.zeros((6, nmu), F32),
        ],
        axis=0,
    )
    spread = dot_nt(density, coulomb[...], lax.Precision.HIGHEST)
    first, second = spread[:, :nmu], spread[:, nmu:]
    u_own = jnp.where(side == 0, first, second)
    u_send[...] = jnp.where(side == 0, second, first)
    u_at = take("recv")
    launch(u_send, u_recv, u_at, device(isdf=1 - side))

    screen()
    back(1)

    arrive(u_recv, u_at)
    potential = u_own + u_recv[...]
    u_real, u_imag = 2.0 * potential[0:1], 2.0 * potential[1:2]
    rs_at = take("recv", 2 * KDEV)
    for k in range(KDEV):
        v_real = vals[REACH, 0, k, :, my_mu].astype(F32)
        v_imag = vals[REACH, 1, k, :, my_mu].astype(F32)
        exchange_real = u_real * v_real - u_imag * v_imag
        exchange_imag = u_real * v_imag + u_imag * v_real
        for channel in (1, 0):
            fields[channel, k] = jnp.concatenate(
                [exchange_real - backs[channel, k, 0], exchange_imag - backs[channel, k, 1]], axis=0
            ).astype(BF16)
            with_real = dot_nt(fields[channel, k], cond[0, k])
            with_imag = dot_nt(fields[channel, k], cond[1, k])
            for part, value in (
                (0, with_real[:nv] + with_imag[nv:]),
                (1, with_real[nv:] - with_imag[:nv]),
            ):
                owns[channel, k, part] = jnp.where(side == 0, value[:, :half], value[:, half:])
                rs_send[channel, k, part] = jnp.where(side == 0, value[:, half:], value[:, :half]).astype(BF16)
            at = channel * KDEV + k
            launch(rs_send.at[channel, k], rs_recv.at[channel, k], rs_at + at, device(isdf=1 - side))

    load_e.wait()
    land_at = take("recv", KDEV)
    land_x_at = take("recv", KDEV)
    cross_at = take("recv", 2 * KDEV)
    back_x = []
    for k in range(KDEV):
        for channel in (1, 0):
            arrive(rs_recv.at[channel, k], rs_at + channel * KDEV + k)
            for part in range(2):
                if channel == 0:
                    amp = xbuf[part, k, :, my_half].astype(F32)
                else:
                    amp = ybuf[part, mirrored[k], :, my_half].astype(F32)
                    amp = -amp if part == 1 else amp
                value = energy[k] * amp + owns[channel, k, part] + rs_recv[channel, k, part].astype(F32)
                if channel == 1 and part == 1:
                    value = -value
                results[channel, k, part] = value.astype(BF16)
            if channel == 1:
                launch(
                    results.at[1, k],
                    land_y.at[pm, k],
                    cross_at + pm * KDEV + k,
                    device(pm=1, ka=across),
                )
            else:
                back_x.append(remote(results.at[0, k], land_x.at[k], land_x_at + k, device(pm=0)))

                @pl.when(pm == 1)
                def _(copy=back_x[-1]):
                    copy.start()

    @pl.when(pm == 0)
    def _():
        for k in range(KDEV):
            out[0, 0, :, k] = results[0, k]
        for k in range(KDEV):
            arrive(land_x.at[k], land_x_at + k)
            out[0, 1, :, k] = land_x[k]

    @pl.when(pm == 1)
    def _():
        for b in range(2):
            for k in range(KDEV):
                arrive(land_y.at[b, k], cross_at + b * KDEV + k)
        for b in range(2):
            for k in range(KDEV):
                out[0, b, :, k] = land_y[b, mirrored[k]]

    for copy in pending:
        copy.wait_send()

    @pl.when(pm == 0)
    def _():
        send_x.wait_send()

    @pl.when(pm == 1)
    def _():
        for copy in send_y + back_x:
            copy.wait_send()


def per_device(grid, amplitudes, conduction, valence, energy, screened, coulomb, mirror, transfer_class):
    nx, nz_hi, nz_lo = grid[:3]
    _, vectors, _, _, nv, nc = amplitudes.shape
    nmu = conduction.shape[3]
    nnu = valence.shape[3]
    half = energy.shape[2]
    pair = (2, KDEV)
    hbm = pl.BlockSpec(memory_space=pl.ANY)
    smem = pl.BlockSpec(memory_space=pltpu.SMEM)
    vmem = pl.BlockSpec(memory_space=pltpu.VMEM)
    return pl.pallas_call(
        functools.partial(kernel, grid),
        out_shape=jax.ShapeDtypeStruct((1, vectors, 2, KDEV, nv, half), BF16),
        in_specs=[hbm] * 6 + [smem] * 2,
        out_specs=vmem,
        scratch_shapes=[
            pltpu.VMEM(conduction.shape, BF16),
            pltpu.VMEM((SLOTS,) + valence.shape, BF16),
            pltpu.VMEM(energy.shape, F32),
            pltpu.VMEM(screened.shape, BF16),
            pltpu.VMEM(coulomb.shape, F32),
            pltpu.VMEM((2, KDEV, nv, nc), BF16),
            pltpu.VMEM((2, KDEV, nv, nc), BF16),
            pltpu.VMEM((2, SLOTS, KDEV, nmu, 2 * nv), BF16),
            pltpu.VMEM((SLOTS * KDEV, 2, nmu, nnu), BF16),
            pltpu.VMEM((KDEV, 2, nmu, nnu), BF16),
            pltpu.VMEM((2, KDEV, 2, nv, nmu), F32),
            pltpu.VMEM((2, KDEV, 2 * nv, nmu), BF16),
            pltpu.VMEM((2, KDEV, 2, nv, half), F32),
            pltpu.VMEM((2, KDEV, 2, nv, half), BF16),
            pltpu.VMEM((2, KDEV, 2, nv, half), BF16),
            pltpu.VMEM((2, KDEV, 2, nv, half), BF16),
            pltpu.VMEM((KDEV, 2, nv, half), BF16),
            pltpu.VMEM((2, KDEV, 2, nv, half), BF16),
            pltpu.VMEM((2 * nx, 8, 128), F32),
            pltpu.VMEM((nz_lo, 8, 128), F32),
            pltpu.VMEM((nz_hi, 8, 128), F32),
            pltpu.VMEM((8, 128), F32),
            pltpu.VMEM((8, nmu), F32),
            pltpu.VMEM((8, nmu), F32),
            pltpu.SemaphoreType.DMA((6,)),
            pltpu.SemaphoreType.DMA((64,)),
            pltpu.SemaphoreType.DMA((64,)),
        ],
        compiler_params=pltpu.CompilerParams(
            collective_id=0, has_side_effects=True, vmem_limit_bytes=40 * 2**20
        ),
    )(amplitudes, conduction, valence, energy, screened, coulomb, mirror, transfer_class)


def solution(mesh):
    blocks = mesh.shape["ka"]
    nz_lo = 4 if blocks >= 128 else 2
    nz_hi = 4 if blocks >= 128 else 1
    nx = blocks // (2 * nz_lo * nz_hi)
    return jax.shard_map(
        functools.partial(per_device, (nx, nz_hi, nz_lo, KDEV * blocks)),
        mesh=mesh,
        in_specs=(
            P("pm", None, None, "ka", None, None),
            P(None, "ka", None, "isdf"),
            P(None, "ka", None, None),
            P("ka", None, "isdf"),
            P(None, None, "isdf", None),
            P(None, "isdf"),
            P("ka"),
            P("ka", None),
        ),
        out_specs=P("pm", None, None, "ka", None, "isdf"),
        check_vma=False,
    )
```

```python
import functools

import jax
import jax.numpy as jnp
from jax import lax
from jax.experimental import pallas as pl
from jax.experimental.pallas import tpu as pltpu
from jax.sharding import PartitionSpec as P

REACH = 2
KDEV = 2
SLOTS = 2 * REACH + 1
BF16 = jnp.bfloat16
F32 = jnp.float32
MESH = pl.DeviceIdType.MESH


def dot_nn(left, right):
    return lax.dot_general(left, right, (((1,), (0,)), ((), ())), preferred_element_type=F32)


def dot_nt(left, right, precision=None):
    return lax.dot_general(
        left, right, (((1,), (1,)), ((), ())), preferred_element_type=F32, precision=precision
    )


def kernel(
    grid,
    amps,
    cond_hbm,
    val_hbm,
    energy_hbm,
    screened_hbm,
    coulomb_hbm,
    mirror,
    classes,
    out,
    cond,
    vals,
    energy,
    screened,
    coulomb,
    xbuf,
    ybuf,
    yhop,
    gbuf,
    mbuf,
    sbuf,
    backs,
    owns,
    rs_send,
    rs_recv,
    results,
    land_x,
    land_y,
    coulomb_high,
    coulomb_low,
    ar_out,
    ar_a,
    ar_b,
    local_sem,
    send_sem,
    recv_sem,
):
    nx, nz, nk = grid
    blocks = nx * nz * 2
    pm = lax.axis_index("pm")
    ka = lax.axis_index("ka")
    side = lax.axis_index("isdf")
    core = ka % 2
    z = (ka // 2) % nz
    x = ka // (2 * nz)
    nv, nc = xbuf.shape[2], xbuf.shape[3]
    nmu = cond.shape[3]
    nnu = vals.shape[4]
    half = nc // 2

    mate = ka + 1 - 2 * core
    above = (ka + REACH) % blocks
    below = (ka + blocks - REACH) % blocks
    across = blocks - 1 - ka

    def ka_of(x_at, z_at, core_at):
        return (x_at * nz + z_at) * 2 + core_at

    a_size = 4 * nx
    a_index = (x * 2 + core) * 2 + side

    def a_peer(step):
        other = (a_index + step) % a_size
        return {"ka": ka_of(other // 4, z, (other // 2) % 2), "isdf": other % 2}

    def b_peer(step):
        return {"ka": ka_of(x, (z + step) % nz, core)}

    here = {"pm": pm, "ka": ka, "isdf": side}

    def device(**change):
        return {**here, **change}

    counter = {"local": 0, "send": 0, "recv": 0}

    def take(kind, count=1):
        first = counter[kind]
        counter[kind] += count
        return first

    def local(src, dst):
        return pltpu.make_async_copy(src, dst, local_sem.at[take("local")])

    pending = []

    def remote(src, dst, recv, target):
        copy = pltpu.make_async_remote_copy(
            src_ref=src,
            dst_ref=dst,
            send_sem=send_sem.at[take("send")],
            recv_sem=recv_sem.at[recv],
            device_id=target,
            device_id_type=MESH,
        )
        return copy

    def launch(src, dst, recv, target):
        copy = remote(src, dst, recv, target)
        copy.start()
        pending.append(copy)

    def arrive(dst, recv):
        pltpu.make_async_remote_copy(
            src_ref=dst,
            dst_ref=dst,
            send_sem=send_sem.at[0],
            recv_sem=recv_sem.at[recv],
            device_id=device(isdf=1 - side),
            device_id_type=MESH,
        ).wait_recv()

    greeted = [
        device(pm=1 - pm),
        device(pm=0, ka=across),
        device(pm=1, ka=across),
        device(isdf=1 - side),
        device(ka=above),
        device(ka=below),
        device(ka=mate),
    ]
    greeted += [device(**a_peer(step)) for step in range(1, a_size)]
    greeted += [device(**b_peer(step)) for step in range(1, nz)]
    barrier = pltpu.get_barrier_semaphore()
    for target in greeted:
        pl.semaphore_signal(barrier, inc=1, device_id=target, device_id_type=MESH)

    load_v = local(val_hbm, vals.at[REACH])
    load_c = local(cond_hbm, cond)
    load_x = local(amps.at[0, 0], xbuf)
    load_s = local(screened_hbm, screened)
    load_k = local(coulomb_hbm, coulomb)
    load_e = local(energy_hbm, energy)
    load_v.start()
    load_c.start()

    @pl.when(pm == 0)
    def _():
        load_x.start()

    load_s.start()
    load_k.start()
    load_e.start()
    pl.semaphore_wait(barrier, len(greeted))

    x_recv = take("recv")
    hop_recv = take("recv", 2)
    y_recv = take("recv", 2)
    y_pass_recv = take("recv", 2)
    v_recv = take("recv", SLOTS)
    g_recv = [take("recv", SLOTS) for _ in range(2)]
    send_x = remote(amps.at[0, 1], xbuf, x_recv, device(pm=1))
    send_hop = [remote(amps.at[0, 0, part, side], yhop.at[part], hop_recv + part, device(pm=0)) for part in range(2)]
    send_y = [
        remote(amps.at[0, 1, part, side], ybuf.at[part, side], y_recv + part, device(ka=across))
        for part in range(2)
    ]
    pass_y = [remote(yhop.at[part], ybuf.at[part, side], y_recv + part, device(ka=across)) for part in range(2)]

    @pl.when(pm == 1)
    def _():
        for part in range(2):
            send_hop[part].start()
            send_y[part].start()

    @pl.when(pm == 0)
    def _():
        send_x.start()
        for part in range(2):
            arrive(yhop.at[part], hop_recv + part)
            pass_y[part].start()

    mate_there = 1 + 2 * core
    mate_here = 3 - 2 * core
    pass_from = 4 - 4 * core
    pass_there = 3 - 2 * core
    passed_here = 1 + 2 * core
    direct_here = 4 * core

    def spread_block(block, landing, recv):
        launch(block, landing.at[0], recv, device(ka=above))
        launch(block, landing.at[SLOTS - 1], recv + SLOTS - 1, device(ka=below))
        launch(block, landing.at[mate_there], recv + mate_there, device(ka=mate))

    def pass_block(landing, recv):
        arrive(landing.at[pass_from], recv + pass_from)
        launch(landing.at[pass_from], landing.at[pass_there], recv + pass_there, device(ka=mate))

    my_mu = pl.ds(pl.multiple_of(side * nmu, nmu), nmu)
    my_half = pl.ds(pl.multiple_of(side * half, half), half)

    def transform(channel, k, z_real, z_imag, sign):
        stack = jnp.concatenate([z_real, z_imag], axis=0)
        with_real = dot_nn(stack, cond[0, k])
        with_imag = dot_nn(stack, cond[1, k])
        g_real = with_real[:nv] - sign * with_imag[nv:]
        g_imag = with_imag[:nv] + sign * with_real[nv:]
        g_all = jnp.concatenate([g_real, g_imag], axis=0)
        gbuf[channel, REACH, k] = jnp.transpose(g_all).astype(BF16)
        v_real = vals[REACH, 0, k, :, my_mu].astype(F32)
        v_imag = vals[REACH, 1, k, :, my_mu].astype(F32)
        rho_real = jnp.sum(v_real * g_real + v_imag * g_imag, axis=0, keepdims=True)
        rho_imag = jnp.sum(v_real * g_imag - v_imag * g_real, axis=0, keepdims=True)
        return rho_real, rho_imag

    def pairs(channel, slot):
        def one(k, carry):
            v_real = vals[slot, 0, k]
            v_imag = vals[slot, 1, k]
            coef = gbuf[channel, slot, k]
            at = slot * KDEV + k
            mbuf[at, 0] = dot_nn(coef, jnp.concatenate([v_real, v_imag], axis=0)).astype(BF16)
            mbuf[at, 1] = dot_nn(coef, jnp.concatenate([-v_imag, v_real], axis=0)).astype(BF16)
            return carry

        lax.fori_loop(0, KDEV, one, 0)

    load_c.wait()
    load_v.wait()

    @pl.when(pm == 0)
    def _():
        load_x.wait()

    @pl.when(pm == 1)
    def _():
        arrive(xbuf, x_recv)

    spread_block(val_hbm, vals, v_recv)
    rho_x = [transform(0, k, xbuf[0, k], xbuf[1, k], 1.0) for k in range(KDEV)]
    spread_block(gbuf.at[0, REACH], gbuf.at[0], g_recv[0])

    def wait_slot(landing, recv, slot):
        arrive(landing.at[slot], recv + slot)

    late = (pass_from, direct_here, passed_here)

    def gather(channel, slots):
        for slot in slots:
            if slot is pass_from:
                if channel == 0:
                    pass_block(vals, v_recv)
                pass_block(gbuf.at[channel], g_recv[channel])
            else:
                if channel == 0:
                    wait_slot(vals, v_recv, slot)
                wait_slot(gbuf.at[channel], g_recv[channel], slot)
            pairs(channel, slot)

    pairs(0, REACH)
    load_k.wait()
    coulomb_high[...] = coulomb[...].astype(BF16)
    coulomb_low[...] = (coulomb[...] - coulomb[...].astype(BF16).astype(F32)).astype(BF16)
    gather(0, (mate_here,))
    for part in range(2):
        arrive(ybuf.at[part, side], y_recv + part)
        launch(ybuf.at[part, side], ybuf.at[part, side], y_pass_recv + part, device(isdf=1 - side))
    for part in range(2):
        arrive(ybuf.at[part, 1 - side], y_pass_recv + part)
    mirrored = [lax.rem(mirror[k], KDEV) for k in range(KDEV)]
    rho_y = [transform(1, k, ybuf[0, mirrored[k]], ybuf[1, mirrored[k]], -1.0) for k in range(KDEV)]
    spread_block(gbuf.at[1, REACH], gbuf.at[1], g_recv[1])

    density = jnp.concatenate(
        [
            sum(part[0] for part in rho_x + rho_y),
            sum(part[1] for part in rho_x + rho_y),
            jnp.zeros((6, nmu), F32),
        ],
        axis=0,
    )
    rest = density - density.astype(BF16).astype(F32)
    both = dot_nt(jnp.concatenate([density, rest], axis=0).astype(BF16), coulomb_high[...])
    share = both[:8] + both[8:] + dot_nt(density.astype(BF16), coulomb_low[...])
    lanes = 128
    pieces = nmu // lanes
    for there in range(2):
        for part in range(2):
            for piece in range(pieces):
                column = there * nmu + piece * lanes
                row = part * pieces + piece
                ar_out[there, pl.ds(row, 1), :] = share[part : part + 1, column : column + lanes]
    a_at = take("recv", a_size)
    for step in range(1, a_size):
        peer = a_peer(step)
        launch(ar_out.at[peer["isdf"]], ar_a.at[a_index], a_at + a_index, device(**peer))
    ar_a[a_index] = ar_out[side]
    b_at = take("recv", nz)

    def second_stage():
        for step in range(1, a_size):
            other = (a_index + step) % a_size
            arrive(ar_a.at[other], a_at + other)
        ar_b[z] = jnp.sum(ar_a[...], axis=0)
        for step in range(1, nz):
            launch(ar_b.at[z], ar_b.at[z], b_at + z, device(**b_peer(step)))

    def last_stage():
        for step in range(1, nz):
            other = (z + step) % nz
            arrive(ar_b.at[other], b_at + other)
        total = 2.0 * jnp.sum(ar_b[...], axis=0)
        return [
            jnp.concatenate([total[part * pieces + i : part * pieces + i + 1] for i in range(pieces)], axis=1)
            for part in range(2)
        ]

    shifts = SLOTS * KDEV + 1
    kinds = [classes[0, (ka * KDEV + nk - (e - SLOTS)) % nk] for e in range(shifts)]

    def screen(k):
        rows = 16

        def one(i, carry):
            row = pl.ds(pl.multiple_of(i * rows, rows), rows)
            for column in range(0, nnu, 128):
                col = pl.ds(column, 128)
                straight = crossed = turned = None
                for t in range(SLOTS * KDEV):
                    kind = kinds[SLOTS * KDEV - 1 + k - t]
                    w_real, w_imag = screened[kind, 0, row, col], screened[kind, 1, row, col]
                    m_real, m_imag = mbuf[t, 0, row, col], mbuf[t, 1, row, col]
                    first, second = w_real * m_real, w_imag * m_imag
                    mixed = w_real * m_imag + w_imag * m_real
                    straight = first if straight is None else straight + first
                    crossed = second if crossed is None else crossed + second
                    turned = mixed if turned is None else turned + mixed
                sbuf[k, 0, row, col] = straight - crossed
                sbuf[k, 1, row, col] = turned
            return carry

        lax.fori_loop(0, nmu // rows, one, 0)

    def back(channel, k):
        v_real, v_imag = vals[REACH, 0, k], vals[REACH, 1, k]
        summed = dot_nt(sbuf[k, 0], jnp.concatenate([v_real, v_imag], axis=0))
        summed = summed + dot_nt(sbuf[k, 1], jnp.concatenate([-v_imag, v_real], axis=0))
        backs[channel, k] = jnp.transpose(summed)

    gather(0, late)
    load_s.wait()
    screen(0)
    back(0, 0)
    second_stage()
    screen(1)
    back(0, 1)

    rs_at = take("recv", 2 * KDEV)
    land_x_at = take("recv", KDEV)
    cross_at = take("recv", 2 * KDEV)
    back_x = []

    def produce(channel, k, u_real, u_imag):
        v_real = vals[REACH, 0, k, :, my_mu].astype(F32)
        v_imag = vals[REACH, 1, k, :, my_mu].astype(F32)
        exchange = jnp.concatenate([u_real * v_real - u_imag * v_imag, u_real * v_imag + u_imag * v_real], axis=0)
        field = (exchange - backs[channel, k]).astype(BF16)
        with_real = dot_nt(field, cond[0, k])
        with_imag = dot_nt(field, cond[1, k])
        for part, value in (
            (0, with_real[:nv] + with_imag[nv:]),
            (1, with_real[nv:] - with_imag[:nv]),
        ):
            owns[channel, k, part] = jnp.where(side == 0, value[:, :half], value[:, half:])
            rs_send[channel, k, part] = jnp.where(side == 0, value[:, half:], value[:, :half]).astype(BF16)
        at = channel * KDEV + k
        launch(rs_send.at[channel, k], rs_recv.at[channel, k], rs_at + at, device(isdf=1 - side))

    def complete(channel, k):
        arrive(rs_recv.at[channel, k], rs_at + channel * KDEV + k)
        for part in range(2):
            if channel == 0:
                amp = xbuf[part, k, :, my_half].astype(F32)
            else:
                amp = ybuf[part, mirrored[k], :, my_half].astype(F32)
                amp = -amp if part == 1 else amp
            value = energy[k] * amp + owns[channel, k, part] + rs_recv[channel, k, part].astype(F32)
            if channel == 1 and part == 1:
                value = -value
            results[channel, k, part] = value.astype(BF16)
        if channel == 1:
            launch(results.at[1, k], land_y.at[pm, k], cross_at + pm * KDEV + k, device(pm=1, ka=across))
        else:
            copy = remote(results.at[0, k], land_x.at[k], land_x_at + k, device(pm=0))
            back_x.append(copy)

            @pl.when(pm == 1)
            def _():
                copy.start()

    pairs(1, REACH)
    gather(1, (mate_here,) + late)
    u_real, u_imag = last_stage()
    produce(0, 0, u_real, u_imag)
    produce(0, 1, u_real, u_imag)
    screen(0)
    back(1, 0)
    produce(1, 0, u_real, u_imag)
    screen(1)
    back(1, 1)
    load_e.wait()
    complete(1, 0)
    produce(1, 1, u_real, u_imag)
    complete(0, 0)
    complete(0, 1)
    complete(1, 1)

    @pl.when(pm == 0)
    def _():
        for k in range(KDEV):
            out[0, 0, :, k] = results[0, k]
        for k in range(KDEV):
            arrive(land_x.at[k], land_x_at + k)
            out[0, 1, :, k] = land_x[k]

    @pl.when(pm == 1)
    def _():
        for b in range(2):
            for k in range(KDEV):
                arrive(land_y.at[b, k], cross_at + b * KDEV + k)
        for b in range(2):
            for k in range(KDEV):
                out[0, b, :, k] = land_y[b, mirrored[k]]

    for copy in pending:
        copy.wait_send()

    @pl.when(pm == 0)
    def _():
        for copy in [send_x] + pass_y:
            copy.wait_send()

    @pl.when(pm == 1)
    def _():
        for copy in send_hop + send_y + back_x:
            copy.wait_send()


def per_device(grid, amplitudes, conduction, valence, energy, screened, coulomb, mirror, transfer_class):
    nx, nz = grid[:2]
    _, vectors, _, _, nv, nc = amplitudes.shape
    nmu = conduction.shape[3]
    nnu = valence.shape[3]
    half = energy.shape[2]
    pair = (2, KDEV)
    hbm = pl.BlockSpec(memory_space=pl.ANY)
    smem = pl.BlockSpec(memory_space=pltpu.SMEM)
    vmem = pl.BlockSpec(memory_space=pltpu.VMEM)
    return pl.pallas_call(
        functools.partial(kernel, grid),
        out_shape=jax.ShapeDtypeStruct((1, vectors, 2, KDEV, nv, half), BF16),
        in_specs=[hbm] * 6 + [smem] * 2,
        out_specs=vmem,
        scratch_shapes=[
            pltpu.VMEM(conduction.shape, BF16),
            pltpu.VMEM((SLOTS,) + valence.shape, BF16),
            pltpu.VMEM(energy.shape, F32),
            pltpu.VMEM(screened.shape, BF16),
            pltpu.VMEM(coulomb.shape, F32),
            pltpu.VMEM((2, KDEV, nv, nc), BF16),
            pltpu.VMEM((2, KDEV, nv, nc), BF16),
            pltpu.VMEM((2, nv, nc), BF16),
            pltpu.VMEM((2, SLOTS, KDEV, nmu, 2 * nv), BF16),
            pltpu.VMEM((SLOTS * KDEV, 2, nmu, nnu), BF16),
            pltpu.VMEM((KDEV, 2, nmu, nnu), BF16),
            pltpu.VMEM((2, KDEV, 2 * nv, nmu), F32),
            pltpu.VMEM((2, KDEV, 2, nv, half), F32),
            pltpu.VMEM((2, KDEV, 2, nv, half), BF16),
            pltpu.VMEM((2, KDEV, 2, nv, half), BF16),
            pltpu.VMEM((2, KDEV, 2, nv, half), BF16),
            pltpu.VMEM((KDEV, 2, nv, half), BF16),
            pltpu.VMEM((2, KDEV, 2, nv, half), BF16),
            pltpu.VMEM(coulomb.shape, BF16),
            pltpu.VMEM(coulomb.shape, BF16),
            pltpu.VMEM((2, 2 * nmu // 128, 128), F32),
            pltpu.VMEM((4 * nx, 2 * nmu // 128, 128), F32),
            pltpu.VMEM((nz, 2 * nmu // 128, 128), F32),
            pltpu.SemaphoreType.DMA((6,)),
            pltpu.SemaphoreType.DMA((80,)),
            pltpu.SemaphoreType.DMA((80,)),
        ],
        compiler_params=pltpu.CompilerParams(
            collective_id=0, has_side_effects=True, vmem_limit_bytes=60 * 2**20
        ),
    )(amplitudes, conduction, valence, energy, screened, coulomb, mirror, transfer_class)


def solution(mesh):
    blocks = mesh.shape["ka"]
    nz = 16 if blocks >= 128 else blocks // 4
    nx = blocks // (2 * nz)
    return jax.shard_map(
        functools.partial(per_device, (nx, nz, KDEV * blocks)),
        mesh=mesh,
        in_specs=(
            P("pm", None, None, "ka", None, None),
            P(None, "ka", None, "isdf"),
            P(None, "ka", None, None),
            P("ka", None, "isdf"),
            P(None, None, "isdf", None),
            P(None, "isdf"),
            P("ka"),
            P("ka", None),
        ),
        out_specs=P("pm", None, None, "ka", None, "isdf"),
        check_vma=False,
    )
```

```python
import functools

import jax
import jax.numpy as jnp
from jax import lax
from jax.experimental import pallas as pl
from jax.experimental.pallas import tpu as pltpu
from jax.sharding import PartitionSpec as P

REACH = 2
KDEV = 2
SLOTS = 2 * REACH + 1
BF16 = jnp.bfloat16
F32 = jnp.float32
MESH = pl.DeviceIdType.MESH


def dot_nn(left, right):
    return lax.dot_general(left, right, (((1,), (0,)), ((), ())), preferred_element_type=F32)


def dot_nt(left, right, precision=None):
    return lax.dot_general(
        left, right, (((1,), (1,)), ((), ())), preferred_element_type=F32, precision=precision
    )


def kernel(
    grid,
    amps,
    cond_hbm,
    val_hbm,
    energy_hbm,
    screened_hbm,
    coulomb_hbm,
    mirror,
    classes,
    out,
    cond,
    vals,
    energy,
    screened,
    coulomb,
    xbuf,
    ybuf,
    yhop,
    gbuf,
    mbuf,
    sbuf,
    backs,
    owns,
    rs_send,
    rs_recv,
    results,
    land_x,
    land_y,
    coulomb_high,
    coulomb_low,
    ar_out,
    ar_a,
    ar_b,
    local_sem,
    send_sem,
    recv_sem,
):
    nx, nz, nk = grid
    blocks = nx * nz * 2
    pm = lax.axis_index("pm")
    ka = lax.axis_index("ka")
    side = lax.axis_index("isdf")
    core = ka % 2
    z = (ka // 2) % nz
    x = ka // (2 * nz)
    nv, nc = xbuf.shape[2], xbuf.shape[3]
    nmu = cond.shape[3]
    nnu = vals.shape[4]
    half = nc // 2

    mate = ka + 1 - 2 * core
    above = (ka + REACH) % blocks
    below = (ka + blocks - REACH) % blocks
    across = blocks - 1 - ka

    def ka_of(x_at, z_at, core_at):
        return (x_at * nz + z_at) * 2 + core_at

    a_size = 4 * nx
    a_index = (x * 2 + core) * 2 + side

    def a_peer(step):
        other = (a_index + step) % a_size
        return {"ka": ka_of(other // 4, z, (other // 2) % 2), "isdf": other % 2}

    def b_peer(step):
        return {"ka": ka_of(x, (z + step) % nz, core)}

    here = {"pm": pm, "ka": ka, "isdf": side}

    def device(**change):
        return {**here, **change}

    counter = {"local": 0, "send": 0, "recv": 0}

    def take(kind, count=1):
        first = counter[kind]
        counter[kind] += count
        return first

    def local(src, dst):
        return pltpu.make_async_copy(src, dst, local_sem.at[take("local")])

    pending = []

    def remote(src, dst, recv, target):
        copy = pltpu.make_async_remote_copy(
            src_ref=src,
            dst_ref=dst,
            send_sem=send_sem.at[take("send")],
            recv_sem=recv_sem.at[recv],
            device_id=target,
            device_id_type=MESH,
        )
        return copy

    def launch(src, dst, recv, target):
        copy = remote(src, dst, recv, target)
        copy.start()
        pending.append(copy)

    def arrive(dst, recv):
        pltpu.make_async_remote_copy(
            src_ref=dst,
            dst_ref=dst,
            send_sem=send_sem.at[0],
            recv_sem=recv_sem.at[recv],
            device_id=device(isdf=1 - side),
            device_id_type=MESH,
        ).wait_recv()

    greeted = [
        device(pm=1 - pm),
        device(pm=0, ka=across),
        device(pm=1, ka=across),
        device(isdf=1 - side),
        device(ka=above),
        device(ka=below),
        device(ka=mate),
    ]
    greeted += [device(**a_peer(step)) for step in range(1, a_size)]
    greeted += [device(**b_peer(step)) for step in range(1, nz)]
    barrier = pltpu.get_barrier_semaphore()
    for target in greeted:
        pl.semaphore_signal(barrier, inc=1, device_id=target, device_id_type=MESH)

    load_v = local(val_hbm, vals.at[REACH])
    load_c = local(cond_hbm, cond)
    load_x = local(amps.at[0, 0], xbuf)
    load_s = local(screened_hbm, screened)
    load_k = local(coulomb_hbm, coulomb)
    load_e = local(energy_hbm, energy)
    load_v.start()
    load_c.start()

    @pl.when(pm == 0)
    def _():
        load_x.start()

    load_s.start()
    load_k.start()
    load_e.start()
    pl.semaphore_wait(barrier, len(greeted))

    x_recv = take("recv")
    hop_recv = take("recv", 2)
    y_recv = take("recv", 2)
    y_pass_recv = take("recv", 2)
    v_recv = take("recv", SLOTS)
    g_recv = [take("recv", SLOTS) for _ in range(1 + KDEV)]
    send_x = remote(amps.at[0, 1], xbuf, x_recv, device(pm=1))
    send_hop = [remote(amps.at[0, 0, part, side], yhop.at[part], hop_recv + part, device(pm=0)) for part in range(2)]
    send_y = [
        remote(amps.at[0, 1, part, side], ybuf.at[part, side], y_recv + part, device(ka=across))
        for part in range(2)
    ]
    pass_y = [remote(yhop.at[part], ybuf.at[part, side], y_recv + part, device(ka=across)) for part in range(2)]

    @pl.when(pm == 1)
    def _():
        for part in range(2):
            send_hop[part].start()
            send_y[part].start()

    @pl.when(pm == 0)
    def _():
        send_x.start()

    mate_there = 1 + 2 * core
    mate_here = 3 - 2 * core
    pass_from = 4 - 4 * core
    pass_there = 3 - 2 * core
    passed_here = 1 + 2 * core
    direct_here = 4 * core

    def spread_block(block, landing, recv):
        launch(block, landing.at[0], recv, device(ka=above))
        launch(block, landing.at[SLOTS - 1], recv + SLOTS - 1, device(ka=below))
        launch(block, landing.at[mate_there], recv + mate_there, device(ka=mate))

    def pass_block(landing, recv):
        arrive(landing.at[pass_from], recv + pass_from)
        launch(landing.at[pass_from], landing.at[pass_there], recv + pass_there, device(ka=mate))

    my_mu = pl.ds(pl.multiple_of(side * nmu, nmu), nmu)
    my_half = pl.ds(pl.multiple_of(side * half, half), half)

    def transform(channel, k, z_real, z_imag, sign):
        stack = jnp.concatenate([z_real, z_imag], axis=0)
        with_real = dot_nn(stack, cond[0, k])
        with_imag = dot_nn(stack, cond[1, k])
        g_real = with_real[:nv] - sign * with_imag[nv:]
        g_imag = with_imag[:nv] + sign * with_real[nv:]
        g_all = jnp.concatenate([g_real, g_imag], axis=0)
        gbuf[channel, REACH, k] = jnp.transpose(g_all).astype(BF16)
        v_real = vals[REACH, 0, k, :, my_mu].astype(F32)
        v_imag = vals[REACH, 1, k, :, my_mu].astype(F32)
        rho_real = jnp.sum(v_real * g_real + v_imag * g_imag, axis=0, keepdims=True)
        rho_imag = jnp.sum(v_real * g_imag - v_imag * g_real, axis=0, keepdims=True)
        return rho_real, rho_imag

    def pairs(channel, slot):
        def one(k, carry):
            v_real = vals[slot, 0, k]
            v_imag = vals[slot, 1, k]
            coef = gbuf[channel, slot, k]
            at = slot * KDEV + k
            mbuf[at, 0] = dot_nn(coef, jnp.concatenate([v_real, v_imag], axis=0)).astype(BF16)
            mbuf[at, 1] = dot_nn(coef, jnp.concatenate([-v_imag, v_real], axis=0)).astype(BF16)
            return carry

        lax.fori_loop(0, KDEV, one, 0)

    load_c.wait()
    load_v.wait()

    @pl.when(pm == 0)
    def _():
        load_x.wait()

    @pl.when(pm == 1)
    def _():
        arrive(xbuf, x_recv)

    rho_x = [transform(0, k, xbuf[0, k], xbuf[1, k], 1.0) for k in range(KDEV)]

    @pl.when(pm == 0)
    def _():
        for part in range(2):
            arrive(yhop.at[part], hop_recv + part)
            pass_y[part].start()

    spread_block(val_hbm, vals, v_recv)
    spread_block(gbuf.at[0, REACH], gbuf.at[0], g_recv[0])
    forwards = [
        remote(ybuf.at[part, side], ybuf.at[part, side], y_pass_recv + part, device(isdf=1 - side))
        for part in range(2)
    ]
    pending.extend(forwards)

    def forward_y():
        for part in range(2):
            arrive(ybuf.at[part, side], y_recv + part)
            forwards[part].start()

    @pl.when(pm == 1)
    def _():
        forward_y()


    def wait_slot(landing, recv, slot):
        arrive(landing.at[slot], recv + slot)

    def screen(k, slots, fresh):
        rows = 16
        terms = []
        for slot in slots:
            for visitor in range(KDEV):
                at = slot * KDEV + visitor
                terms.append((at, classes[0, (ka * KDEV + nk - (SLOTS - 1) - k + at) % nk]))

        def one(i, carry):
            row = pl.ds(pl.multiple_of(i * rows, rows), rows)
            for column in range(0, nnu, 128):
                col = pl.ds(column, 128)
                straight = None if fresh else sbuf[k, 0, row, col]
                turned = None if fresh else sbuf[k, 1, row, col]
                crossed = None
                for at, kind in terms:
                    w_real, w_imag = screened[kind, 0, row, col], screened[kind, 1, row, col]
                    m_real, m_imag = mbuf[at, 0, row, col], mbuf[at, 1, row, col]
                    first, second = w_real * m_real, w_imag * m_imag
                    mixed = w_real * m_imag + w_imag * m_real
                    straight = first if straight is None else straight + first
                    crossed = second if crossed is None else crossed + second
                    turned = mixed if turned is None else turned + mixed
                sbuf[k, 0, row, col] = straight - crossed
                sbuf[k, 1, row, col] = turned
            return carry

        lax.fori_loop(0, nmu // rows, one, 0)

    late = (pass_from, direct_here, passed_here)

    def gather(channel, slots):
        flows = [(gbuf.at[1, :, k], g_recv[1 + k]) for k in range(KDEV)]
        if channel == 0:
            flows = [(vals, v_recv), (gbuf.at[0], g_recv[0])]
        for slot in slots:
            for landing, recv in flows:
                if slot is pass_from:
                    pass_block(landing, recv)
                else:
                    wait_slot(landing, recv, slot)
            pairs(channel, slot)

    pairs(0, REACH)
    load_k.wait()
    coulomb_high[...] = coulomb[...].astype(BF16)
    coulomb_low[...] = (coulomb[...] - coulomb[...].astype(BF16).astype(F32)).astype(BF16)
    gather(0, (mate_here,))
    load_s.wait()
    for k in range(KDEV):
        screen(k, (REACH, mate_here), True)

    @pl.when(pm == 0)
    def _():
        forward_y()

    for part in range(2):
        arrive(ybuf.at[part, 1 - side], y_pass_recv + part)
    mirrored = [lax.rem(mirror[k], KDEV) for k in range(KDEV)]
    rho_y = []
    for k in range(KDEV):
        rho_y.append(transform(1, k, ybuf[0, mirrored[k]], ybuf[1, mirrored[k]], -1.0))
        spread_block(gbuf.at[1, REACH, k], gbuf.at[1, :, k], g_recv[1 + k])

    density = jnp.concatenate(
        [
            sum(part[0] for part in rho_x + rho_y),
            sum(part[1] for part in rho_x + rho_y),
            jnp.zeros((6, nmu), F32),
        ],
        axis=0,
    )
    rest = density - density.astype(BF16).astype(F32)
    both = dot_nt(jnp.concatenate([density, rest], axis=0).astype(BF16), coulomb_high[...])
    share = both[:8] + both[8:] + dot_nt(density.astype(BF16), coulomb_low[...])
    lanes = 128
    pieces = nmu // lanes
    for there in range(2):
        for part in range(2):
            for piece in range(pieces):
                column = there * nmu + piece * lanes
                row = part * pieces + piece
                ar_out[there, pl.ds(row, 1), :] = share[part : part + 1, column : column + lanes]
    a_at = take("recv", a_size)
    for step in range(1, a_size):
        peer = a_peer(step)
        launch(ar_out.at[peer["isdf"]], ar_a.at[a_index], a_at + a_index, device(**peer))
    ar_a[a_index] = ar_out[side]
    b_at = take("recv", nz)

    def second_stage():
        for step in range(1, a_size):
            other = (a_index + step) % a_size
            arrive(ar_a.at[other], a_at + other)
        ar_b[z] = jnp.sum(ar_a[...], axis=0)
        for step in range(1, nz):
            launch(ar_b.at[z], ar_b.at[z], b_at + z, device(**b_peer(step)))

    def last_stage():
        for step in range(1, nz):
            other = (z + step) % nz
            arrive(ar_b.at[other], b_at + other)
        total = 2.0 * jnp.sum(ar_b[...], axis=0)
        return [
            jnp.concatenate([total[part * pieces + i : part * pieces + i + 1] for i in range(pieces)], axis=1)
            for part in range(2)
        ]

    def back(channel, k):
        v_real, v_imag = vals[REACH, 0, k], vals[REACH, 1, k]
        summed = dot_nt(sbuf[k, 0], jnp.concatenate([v_real, v_imag], axis=0))
        summed = summed + dot_nt(sbuf[k, 1], jnp.concatenate([-v_imag, v_real], axis=0))
        backs[channel, k] = jnp.transpose(summed)

    gather(0, late)
    screen(0, late, False)
    back(0, 0)
    second_stage()
    screen(1, late, False)
    back(0, 1)

    rs_at = take("recv", 2 * KDEV)
    land_x_at = take("recv", KDEV)
    cross_at = take("recv", 2 * KDEV)
    back_x = []

    def produce(channel, k, u_real, u_imag):
        v_real = vals[REACH, 0, k, :, my_mu].astype(F32)
        v_imag = vals[REACH, 1, k, :, my_mu].astype(F32)
        exchange = jnp.concatenate([u_real * v_real - u_imag * v_imag, u_real * v_imag + u_imag * v_real], axis=0)
        field = (exchange - backs[channel, k]).astype(BF16)
        with_real = dot_nt(field, cond[0, k])
        with_imag = dot_nt(field, cond[1, k])
        for part, value in (
            (0, with_real[:nv] + with_imag[nv:]),
            (1, with_real[nv:] - with_imag[:nv]),
        ):
            owns[channel, k, part] = jnp.where(side == 0, value[:, :half], value[:, half:])
            rs_send[channel, k, part] = jnp.where(side == 0, value[:, half:], value[:, :half]).astype(BF16)
        at = channel * KDEV + k
        launch(rs_send.at[channel, k], rs_recv.at[channel, k], rs_at + at, device(isdf=1 - side))

    def complete(channel, k):
        arrive(rs_recv.at[channel, k], rs_at + channel * KDEV + k)
        for part in range(2):
            if channel == 0:
                amp = xbuf[part, k, :, my_half].astype(F32)
            else:
                amp = ybuf[part, mirrored[k], :, my_half].astype(F32)
                amp = -amp if part == 1 else amp
            value = energy[k] * amp + owns[channel, k, part] + rs_recv[channel, k, part].astype(F32)
            if channel == 1 and part == 1:
                value = -value
            results[channel, k, part] = value.astype(BF16)
        if channel == 1:
            launch(results.at[1, k], land_y.at[pm, k], cross_at + pm * KDEV + k, device(pm=1, ka=across))
        else:
            copy = remote(results.at[0, k], land_x.at[k], land_x_at + k, device(pm=0))
            back_x.append(copy)

            @pl.when(pm == 1)
            def _():
                copy.start()

    pairs(1, REACH)
    gather(1, (mate_here,) + late)
    everything = tuple(range(SLOTS))
    screen(0, everything, True)
    back(1, 0)
    u_real, u_imag = last_stage()
    produce(1, 0, u_real, u_imag)
    screen(1, everything, True)
    back(1, 1)
    produce(1, 1, u_real, u_imag)
    load_e.wait()
    complete(1, 0)
    produce(0, 0, u_real, u_imag)
    produce(0, 1, u_real, u_imag)
    complete(1, 1)
    complete(0, 0)
    complete(0, 1)

    @pl.when(pm == 0)
    def _():
        for k in range(KDEV):
            out[0, 0, :, k] = results[0, k]
        for k in range(KDEV):
            arrive(land_x.at[k], land_x_at + k)
            out[0, 1, :, k] = land_x[k]

    @pl.when(pm == 1)
    def _():
        for b in range(2):
            for k in range(KDEV):
                arrive(land_y.at[b, k], cross_at + b * KDEV + k)
        for b in range(2):
            for k in range(KDEV):
                out[0, b, :, k] = land_y[b, mirrored[k]]

    for copy in pending:
        copy.wait_send()

    @pl.when(pm == 0)
    def _():
        for copy in [send_x] + pass_y:
            copy.wait_send()

    @pl.when(pm == 1)
    def _():
        for copy in send_hop + send_y + back_x:
            copy.wait_send()


def per_device(grid, amplitudes, conduction, valence, energy, screened, coulomb, mirror, transfer_class):
    nx, nz = grid[:2]
    _, vectors, _, _, nv, nc = amplitudes.shape
    nmu = conduction.shape[3]
    nnu = valence.shape[3]
    half = energy.shape[2]
    pair = (2, KDEV)
    hbm = pl.BlockSpec(memory_space=pl.ANY)
    smem = pl.BlockSpec(memory_space=pltpu.SMEM)
    vmem = pl.BlockSpec(memory_space=pltpu.VMEM)
    return pl.pallas_call(
        functools.partial(kernel, grid),
        out_shape=jax.ShapeDtypeStruct((1, vectors, 2, KDEV, nv, half), BF16),
        in_specs=[hbm] * 6 + [smem] * 2,
        out_specs=vmem,
        scratch_shapes=[
            pltpu.VMEM(conduction.shape, BF16),
            pltpu.VMEM((SLOTS,) + valence.shape, BF16),
            pltpu.VMEM(energy.shape, F32),
            pltpu.VMEM(screened.shape, BF16),
            pltpu.VMEM(coulomb.shape, F32),
            pltpu.VMEM((2, KDEV, nv, nc), BF16),
            pltpu.VMEM((2, KDEV, nv, nc), BF16),
            pltpu.VMEM((2, nv, nc), BF16),
            pltpu.VMEM((2, SLOTS, KDEV, nmu, 2 * nv), BF16),
            pltpu.VMEM((SLOTS * KDEV, 2, nmu, nnu), BF16),
            pltpu.VMEM((KDEV, 2, nmu, nnu), BF16),
            pltpu.VMEM((2, KDEV, 2 * nv, nmu), F32),
            pltpu.VMEM((2, KDEV, 2, nv, half), F32),
            pltpu.VMEM((2, KDEV, 2, nv, half), BF16),
            pltpu.VMEM((2, KDEV, 2, nv, half), BF16),
            pltpu.VMEM((2, KDEV, 2, nv, half), BF16),
            pltpu.VMEM((KDEV, 2, nv, half), BF16),
            pltpu.VMEM((2, KDEV, 2, nv, half), BF16),
            pltpu.VMEM(coulomb.shape, BF16),
            pltpu.VMEM(coulomb.shape, BF16),
            pltpu.VMEM((2, 2 * nmu // 128, 128), F32),
            pltpu.VMEM((4 * nx, 2 * nmu // 128, 128), F32),
            pltpu.VMEM((nz, 2 * nmu // 128, 128), F32),
            pltpu.SemaphoreType.DMA((6,)),
            pltpu.SemaphoreType.DMA((80,)),
            pltpu.SemaphoreType.DMA((80,)),
        ],
        compiler_params=pltpu.CompilerParams(
            collective_id=0, has_side_effects=True, vmem_limit_bytes=60 * 2**20
        ),
    )(amplitudes, conduction, valence, energy, screened, coulomb, mirror, transfer_class)


def solution(mesh):
    blocks = mesh.shape["ka"]
    nz = 16 if blocks >= 128 else blocks // 4
    nx = blocks // (2 * nz)
    return jax.shard_map(
        functools.partial(per_device, (nx, nz, KDEV * blocks)),
        mesh=mesh,
        in_specs=(
            P("pm", None, None, "ka", None, None),
            P(None, "ka", None, "isdf"),
            P(None, "ka", None, None),
            P("ka", None, "isdf"),
            P(None, None, "isdf", None),
            P(None, "isdf"),
            P("ka"),
            P("ka", None),
        ),
        out_specs=P("pm", None, None, "ka", None, "isdf"),
        check_vma=False,
    )
```

```python
import functools

import jax
import jax.numpy as jnp
from jax import lax
from jax.experimental import pallas as pl
from jax.experimental.pallas import tpu as pltpu
from jax.sharding import PartitionSpec as P

REACH = 2
KDEV = 2
SLOTS = 2 * REACH + 1
BF16 = jnp.bfloat16
F32 = jnp.float32
MESH = pl.DeviceIdType.MESH


def dot_nn(left, right):
    return lax.dot_general(left, right, (((1,), (0,)), ((), ())), preferred_element_type=F32)


def dot_nt(left, right, precision=None):
    return lax.dot_general(
        left, right, (((1,), (1,)), ((), ())), preferred_element_type=F32, precision=precision
    )


def kernel(
    grid,
    amps,
    cond_hbm,
    val_hbm,
    energy_hbm,
    screened_hbm,
    coulomb_hbm,
    mirror,
    classes,
    out,
    cond,
    vals,
    energy,
    screened,
    coulomb,
    xbuf,
    ybuf,
    yhop,
    gbuf,
    mbuf,
    sbuf,
    backs,
    owns,
    rs_send,
    rs_recv,
    results,
    land_x,
    land_y,
    coulomb_high,
    coulomb_low,
    ar_out,
    ar_a,
    ar_b,
    local_sem,
    send_sem,
    recv_sem,
):
    nx, nz, nk = grid
    blocks = nx * nz * 2
    pm = lax.axis_index("pm")
    ka = lax.axis_index("ka")
    side = lax.axis_index("isdf")
    core = ka % 2
    z = (ka // 2) % nz
    x = ka // (2 * nz)
    nv, nc = xbuf.shape[2], xbuf.shape[3]
    nmu = cond.shape[3]
    nnu = vals.shape[4]
    half = nc // 2

    mate = ka + 1 - 2 * core
    above = (ka + REACH) % blocks
    below = (ka + blocks - REACH) % blocks
    across = blocks - 1 - ka

    def ka_of(x_at, z_at, core_at):
        return (x_at * nz + z_at) * 2 + core_at

    a_size = 4 * nx
    a_index = (x * 2 + core) * 2 + side

    def a_peer(step):
        other = (a_index + step) % a_size
        return {"ka": ka_of(other // 4, z, (other // 2) % 2), "isdf": other % 2}

    def b_peer(step):
        return {"ka": ka_of(x, (z + step) % nz, core)}

    here = {"pm": pm, "ka": ka, "isdf": side}

    def device(**change):
        return {**here, **change}

    counter = {"local": 0, "send": 0, "recv": 0}

    def take(kind, count=1):
        first = counter[kind]
        counter[kind] += count
        return first

    def local(src, dst):
        return pltpu.make_async_copy(src, dst, local_sem.at[take("local")])

    pending = []

    def remote(src, dst, recv, target):
        copy = pltpu.make_async_remote_copy(
            src_ref=src,
            dst_ref=dst,
            send_sem=send_sem.at[take("send")],
            recv_sem=recv_sem.at[recv],
            device_id=target,
            device_id_type=MESH,
        )
        return copy

    def launch(src, dst, recv, target):
        copy = remote(src, dst, recv, target)
        copy.start()
        pending.append(copy)

    def arrive(dst, recv):
        pltpu.make_async_remote_copy(
            src_ref=dst,
            dst_ref=dst,
            send_sem=send_sem.at[0],
            recv_sem=recv_sem.at[recv],
            device_id=device(isdf=1 - side),
            device_id_type=MESH,
        ).wait_recv()

    greeted = [
        device(pm=1 - pm),
        device(pm=0, ka=across),
        device(pm=1, ka=across),
        device(isdf=1 - side),
        device(ka=above),
        device(ka=below),
        device(ka=mate),
    ]
    greeted += [device(**a_peer(step)) for step in range(1, a_size)]
    greeted += [device(**b_peer(step)) for step in range(1, nz)]
    barrier = pltpu.get_barrier_semaphore()
    for target in greeted:
        pl.semaphore_signal(barrier, inc=1, device_id=target, device_id_type=MESH)

    load_v = local(val_hbm, vals.at[REACH])
    load_c = local(cond_hbm, cond)
    load_x = local(amps.at[0, 0], xbuf)
    load_s = local(screened_hbm, screened)
    load_k = local(coulomb_hbm, coulomb)
    load_e = local(energy_hbm, energy)
    load_v.start()
    load_c.start()

    @pl.when(pm == 0)
    def _():
        load_x.start()

    load_s.start()
    load_k.start()
    load_e.start()
    pl.semaphore_wait(barrier, len(greeted))

    x_recv = take("recv")
    hop_recv = take("recv", 2)
    y_recv = take("recv", 2)
    y_pass_recv = take("recv", 2)
    v_recv = take("recv", SLOTS)
    g_recv = [take("recv", SLOTS) for _ in range(1 + KDEV)]
    send_x = remote(amps.at[0, 1], xbuf, x_recv, device(pm=1))
    send_hop = [remote(amps.at[0, 0, part, side], yhop.at[part], hop_recv + part, device(pm=0)) for part in range(2)]
    send_y = [
        remote(amps.at[0, 1, part, side], ybuf.at[part, side], y_recv + part, device(ka=across))
        for part in range(2)
    ]
    pass_y = [remote(yhop.at[part], ybuf.at[part, side], y_recv + part, device(ka=across)) for part in range(2)]

    @pl.when(pm == 1)
    def _():
        for part in range(2):
            send_hop[part].start()
            send_y[part].start()

    @pl.when(pm == 0)
    def _():
        send_x.start()

    mate_there = 1 + 2 * core
    mate_here = 3 - 2 * core
    pass_from = 4 - 4 * core
    pass_there = 3 - 2 * core
    passed_here = 1 + 2 * core
    direct_here = 4 * core

    def spread_block(block, landing, recv):
        launch(block, landing.at[0], recv, device(ka=above))
        launch(block, landing.at[SLOTS - 1], recv + SLOTS - 1, device(ka=below))
        launch(block, landing.at[mate_there], recv + mate_there, device(ka=mate))

    def pass_block(landing, recv):
        arrive(landing.at[pass_from], recv + pass_from)
        launch(landing.at[pass_from], landing.at[pass_there], recv + pass_there, device(ka=mate))

    my_mu = pl.ds(pl.multiple_of(side * nmu, nmu), nmu)
    my_half = pl.ds(pl.multiple_of(side * half, half), half)

    def transform(channel, k, z_real, z_imag, sign):
        stack = jnp.concatenate([z_real, z_imag], axis=0)
        with_real = dot_nn(stack, cond[0, k])
        with_imag = dot_nn(stack, cond[1, k])
        g_real = with_real[:nv] - sign * with_imag[nv:]
        g_imag = with_imag[:nv] + sign * with_real[nv:]
        g_all = jnp.concatenate([g_real, g_imag], axis=0)
        gbuf[channel, REACH, k] = jnp.transpose(g_all).astype(BF16)
        v_real = vals[REACH, 0, k, :, my_mu].astype(F32)
        v_imag = vals[REACH, 1, k, :, my_mu].astype(F32)
        rho_real = jnp.sum(v_real * g_real + v_imag * g_imag, axis=0, keepdims=True)
        rho_imag = jnp.sum(v_real * g_imag - v_imag * g_real, axis=0, keepdims=True)
        return rho_real, rho_imag

    def pairs(channel, slot):
        def one(k, carry):
            v_real = vals[slot, 0, k]
            v_imag = vals[slot, 1, k]
            coef = gbuf[channel, slot, k]
            at = slot * KDEV + k
            mbuf[at, 0] = dot_nn(coef, jnp.concatenate([v_real, v_imag], axis=0)).astype(BF16)
            mbuf[at, 1] = dot_nn(coef, jnp.concatenate([-v_imag, v_real], axis=0)).astype(BF16)
            return carry

        lax.fori_loop(0, KDEV, one, 0)

    load_c.wait()
    load_v.wait()

    @pl.when(pm == 0)
    def _():
        load_x.wait()

    @pl.when(pm == 1)
    def _():
        arrive(xbuf, x_recv)

    rho_x = [transform(0, k, xbuf[0, k], xbuf[1, k], 1.0) for k in range(KDEV)]

    @pl.when(pm == 0)
    def _():
        for part in range(2):
            arrive(yhop.at[part], hop_recv + part)
            pass_y[part].start()

    spread_block(val_hbm, vals, v_recv)
    spread_block(gbuf.at[0, REACH], gbuf.at[0], g_recv[0])
    forwards = [
        remote(ybuf.at[part, side], ybuf.at[part, side], y_pass_recv + part, device(isdf=1 - side))
        for part in range(2)
    ]
    pending.extend(forwards)

    def forward_y():
        for part in range(2):
            arrive(ybuf.at[part, side], y_recv + part)
            forwards[part].start()

    @pl.when(pm == 1)
    def _():
        forward_y()


    def wait_slot(landing, recv, slot):
        arrive(landing.at[slot], recv + slot)

    def screen(k, slots, fresh):
        rows = 16
        terms = []
        for slot in slots:
            for visitor in range(KDEV):
                at = slot * KDEV + visitor
                terms.append((at, classes[0, (ka * KDEV + nk - (SLOTS - 1) - k + at) % nk]))

        def one(i, carry):
            row = pl.ds(pl.multiple_of(i * rows, rows), rows)
            for column in range(0, nnu, 128):
                col = pl.ds(column, 128)
                straight = None if fresh else sbuf[k, 0, row, col]
                turned = None if fresh else sbuf[k, 1, row, col]
                crossed = None
                for at, kind in terms:
                    w_real, w_imag = screened[kind, 0, row, col], screened[kind, 1, row, col]
                    m_real, m_imag = mbuf[at, 0, row, col], mbuf[at, 1, row, col]
                    first, second = w_real * m_real, w_imag * m_imag
                    mixed = w_real * m_imag + w_imag * m_real
                    straight = first if straight is None else straight + first
                    crossed = second if crossed is None else crossed + second
                    turned = mixed if turned is None else turned + mixed
                sbuf[k, 0, row, col] = straight - crossed
                sbuf[k, 1, row, col] = turned
            return carry

        lax.fori_loop(0, nmu // rows, one, 0)

    late = (pass_from, direct_here, passed_here)

    def gather(channel, slots):
        flows = [(gbuf.at[1, :, k], g_recv[1 + k]) for k in range(KDEV)]
        if channel == 0:
            flows = [(vals, v_recv), (gbuf.at[0], g_recv[0])]
        for slot in slots:
            for landing, recv in flows:
                if slot is pass_from:
                    pass_block(landing, recv)
                else:
                    wait_slot(landing, recv, slot)
            pairs(channel, slot)

    pairs(0, REACH)
    load_k.wait()
    coulomb_high[...] = coulomb[...].astype(BF16)
    coulomb_low[...] = (coulomb[...] - coulomb[...].astype(BF16).astype(F32)).astype(BF16)
    gather(0, (mate_here,))
    load_s.wait()
    for k in range(KDEV):
        screen(k, (REACH, mate_here), True)

    @pl.when(pm == 0)
    def _():
        forward_y()

    for part in range(2):
        arrive(ybuf.at[part, 1 - side], y_pass_recv + part)
    mirrored = [lax.rem(mirror[k], KDEV) for k in range(KDEV)]
    rho_y = []
    for k in range(KDEV):
        rho_y.append(transform(1, k, ybuf[0, mirrored[k]], ybuf[1, mirrored[k]], -1.0))
        spread_block(gbuf.at[1, REACH, k], gbuf.at[1, :, k], g_recv[1 + k])

    density = jnp.concatenate(
        [
            sum(part[0] for part in rho_x + rho_y),
            sum(part[1] for part in rho_x + rho_y),
            jnp.zeros((6, nmu), F32),
        ],
        axis=0,
    )
    rest = density - density.astype(BF16).astype(F32)
    both = dot_nt(jnp.concatenate([density, rest], axis=0).astype(BF16), coulomb_high[...])
    share = both[:8] + both[8:] + dot_nt(density.astype(BF16), coulomb_low[...])
    lanes = 128
    pieces = nmu // lanes
    for there in range(2):
        for part in range(2):
            for piece in range(pieces):
                column = there * nmu + piece * lanes
                row = part * pieces + piece
                ar_out[there, pl.ds(row, 1), :] = share[part : part + 1, column : column + lanes]
    a_at = take("recv", a_size)
    for step in range(1, a_size):
        peer = a_peer(step)
        launch(ar_out.at[peer["isdf"]], ar_a.at[a_index], a_at + a_index, device(**peer))
    ar_a[a_index] = ar_out[side]
    b_at = take("recv", nz)

    def second_stage():
        for step in range(1, a_size):
            other = (a_index + step) % a_size
            arrive(ar_a.at[other], a_at + other)
        ar_b[z] = jnp.sum(ar_a[...], axis=0)
        for step in range(1, nz):
            launch(ar_b.at[z], ar_b.at[z], b_at + z, device(**b_peer(step)))

    def last_stage():
        for step in range(1, nz):
            other = (z + step) % nz
            arrive(ar_b.at[other], b_at + other)
        total = 2.0 * jnp.sum(ar_b[...], axis=0)
        return [
            jnp.concatenate([total[part * pieces + i : part * pieces + i + 1] for i in range(pieces)], axis=1)
            for part in range(2)
        ]

    def back(channel, k):
        v_real, v_imag = vals[REACH, 0, k], vals[REACH, 1, k]
        summed = dot_nt(sbuf[k, 0], jnp.concatenate([v_real, v_imag], axis=0))
        summed = summed + dot_nt(sbuf[k, 1], jnp.concatenate([-v_imag, v_real], axis=0))
        backs[channel, k] = jnp.transpose(summed)

    gather(0, late)
    screen(0, late, False)
    back(0, 0)
    second_stage()
    screen(1, late, False)
    back(0, 1)

    rs_at = take("recv", 2 * KDEV)
    land_x_at = take("recv", KDEV)
    cross_at = take("recv", 2 * KDEV)
    back_x = []

    def produce(channel, k, u_real, u_imag):
        v_real = vals[REACH, 0, k, :, my_mu].astype(F32)
        v_imag = vals[REACH, 1, k, :, my_mu].astype(F32)
        exchange = jnp.concatenate([u_real * v_real - u_imag * v_imag, u_real * v_imag + u_imag * v_real], axis=0)
        field = (exchange - backs[channel, k]).astype(BF16)
        with_real = dot_nt(field, cond[0, k])
        with_imag = dot_nt(field, cond[1, k])
        for part, value in (
            (0, with_real[:nv] + with_imag[nv:]),
            (1, with_real[nv:] - with_imag[:nv]),
        ):
            owns[channel, k, part] = jnp.where(side == 0, value[:, :half], value[:, half:])
            rs_send[channel, k, part] = jnp.where(side == 0, value[:, half:], value[:, :half]).astype(BF16)
        at = channel * KDEV + k
        launch(rs_send.at[channel, k], rs_recv.at[channel, k], rs_at + at, device(isdf=1 - side))

    def complete(channel, k):
        arrive(rs_recv.at[channel, k], rs_at + channel * KDEV + k)
        for part in range(2):
            if channel == 0:
                amp = xbuf[part, k, :, my_half].astype(F32)
            else:
                amp = ybuf[part, mirrored[k], :, my_half].astype(F32)
                amp = -amp if part == 1 else amp
            value = energy[k] * amp + owns[channel, k, part] + rs_recv[channel, k, part].astype(F32)
            if channel == 1 and part == 1:
                value = -value
            results[channel, k, part] = value.astype(BF16)
        if channel == 1:
            launch(results.at[1, k], land_y.at[pm, k], cross_at + pm * KDEV + k, device(pm=1, ka=across))
        else:
            copy = remote(results.at[0, k], land_x.at[k], land_x_at + k, device(pm=0))
            back_x.append(copy)

            @pl.when(pm == 1)
            def _():
                copy.start()

    pairs(1, REACH)
    gather(1, (mate_here,))
    for k in range(KDEV):
        screen(k, (REACH, mate_here), True)
    gather(1, late)
    screen(0, late, False)
    back(1, 0)
    u_real, u_imag = last_stage()
    produce(1, 0, u_real, u_imag)
    screen(1, late, False)
    back(1, 1)
    produce(1, 1, u_real, u_imag)
    load_e.wait()
    complete(1, 0)
    produce(0, 0, u_real, u_imag)
    produce(0, 1, u_real, u_imag)
    complete(1, 1)
    complete(0, 0)
    complete(0, 1)

    @pl.when(pm == 0)
    def _():
        for k in range(KDEV):
            out[0, 0, :, k] = results[0, k]
        for k in range(KDEV):
            arrive(land_x.at[k], land_x_at + k)
            out[0, 1, :, k] = land_x[k]

    @pl.when(pm == 1)
    def _():
        for b in range(2):
            for k in range(KDEV):
                arrive(land_y.at[b, k], cross_at + b * KDEV + k)
        for b in range(2):
            for k in range(KDEV):
                out[0, b, :, k] = land_y[b, mirrored[k]]

    for copy in pending:
        copy.wait_send()

    @pl.when(pm == 0)
    def _():
        for copy in [send_x] + pass_y:
            copy.wait_send()

    @pl.when(pm == 1)
    def _():
        for copy in send_hop + send_y + back_x:
            copy.wait_send()


def per_device(grid, amplitudes, conduction, valence, energy, screened, coulomb, mirror, transfer_class):
    nx, nz = grid[:2]
    _, vectors, _, _, nv, nc = amplitudes.shape
    nmu = conduction.shape[3]
    nnu = valence.shape[3]
    half = energy.shape[2]
    pair = (2, KDEV)
    hbm = pl.BlockSpec(memory_space=pl.ANY)
    smem = pl.BlockSpec(memory_space=pltpu.SMEM)
    vmem = pl.BlockSpec(memory_space=pltpu.VMEM)
    return pl.pallas_call(
        functools.partial(kernel, grid),
        out_shape=jax.ShapeDtypeStruct((1, vectors, 2, KDEV, nv, half), BF16),
        in_specs=[hbm] * 6 + [smem] * 2,
        out_specs=vmem,
        scratch_shapes=[
            pltpu.VMEM(conduction.shape, BF16),
            pltpu.VMEM((SLOTS,) + valence.shape, BF16),
            pltpu.VMEM(energy.shape, F32),
            pltpu.VMEM(screened.shape, BF16),
            pltpu.VMEM(coulomb.shape, F32),
            pltpu.VMEM((2, KDEV, nv, nc), BF16),
            pltpu.VMEM((2, KDEV, nv, nc), BF16),
            pltpu.VMEM((2, nv, nc), BF16),
            pltpu.VMEM((2, SLOTS, KDEV, nmu, 2 * nv), BF16),
            pltpu.VMEM((SLOTS * KDEV, 2, nmu, nnu), BF16),
            pltpu.VMEM((KDEV, 2, nmu, nnu), BF16),
            pltpu.VMEM((2, KDEV, 2 * nv, nmu), F32),
            pltpu.VMEM((2, KDEV, 2, nv, half), F32),
            pltpu.VMEM((2, KDEV, 2, nv, half), BF16),
            pltpu.VMEM((2, KDEV, 2, nv, half), BF16),
            pltpu.VMEM((2, KDEV, 2, nv, half), BF16),
            pltpu.VMEM((KDEV, 2, nv, half), BF16),
            pltpu.VMEM((2, KDEV, 2, nv, half), BF16),
            pltpu.VMEM(coulomb.shape, BF16),
            pltpu.VMEM(coulomb.shape, BF16),
            pltpu.VMEM((2, 2 * nmu // 128, 128), F32),
            pltpu.VMEM((4 * nx, 2 * nmu // 128, 128), F32),
            pltpu.VMEM((nz, 2 * nmu // 128, 128), F32),
            pltpu.SemaphoreType.DMA((6,)),
            pltpu.SemaphoreType.DMA((80,)),
            pltpu.SemaphoreType.DMA((80,)),
        ],
        compiler_params=pltpu.CompilerParams(
            collective_id=0, has_side_effects=True, vmem_limit_bytes=60 * 2**20
        ),
    )(amplitudes, conduction, valence, energy, screened, coulomb, mirror, transfer_class)


def solution(mesh):
    blocks = mesh.shape["ka"]
    nz = 16 if blocks >= 128 else blocks // 4
    nx = blocks // (2 * nz)
    return jax.shard_map(
        functools.partial(per_device, (nx, nz, KDEV * blocks)),
        mesh=mesh,
        in_specs=(
            P("pm", None, None, "ka", None, None),
            P(None, "ka", None, "isdf"),
            P(None, "ka", None, None),
            P("ka", None, "isdf"),
            P(None, None, "isdf", None),
            P(None, "isdf"),
            P("ka"),
            P("ka", None),
        ),
        out_specs=P("pm", None, None, "ka", None, "isdf"),
        check_vma=False,
    )
```

```python
import functools

import jax
import jax.numpy as jnp
from jax import lax
from jax.experimental import pallas as pl
from jax.experimental.pallas import tpu as pltpu
from jax.sharding import PartitionSpec as P

REACH = 2
KDEV = 2
SLOTS = 2 * REACH + 1
BF16 = jnp.bfloat16
F32 = jnp.float32
MESH = pl.DeviceIdType.MESH


def dot_nn(left, right):
    return lax.dot_general(left, right, (((1,), (0,)), ((), ())), preferred_element_type=F32)


def dot_nt(left, right, precision=None):
    return lax.dot_general(
        left, right, (((1,), (1,)), ((), ())), preferred_element_type=F32, precision=precision
    )


def kernel(
    grid,
    amps,
    cond_hbm,
    val_hbm,
    energy_hbm,
    screened_hbm,
    coulomb_hbm,
    mirror,
    classes,
    out,
    cond,
    vals,
    energy,
    screened,
    coulomb,
    xbuf,
    ybuf,
    yhop,
    gbuf,
    mbuf,
    sbuf,
    backs,
    owns,
    rs_send,
    rs_recv,
    results,
    land_x,
    land_y,
    coulomb_high,
    coulomb_low,
    ar_out,
    ar_a,
    ar_b,
    local_sem,
    send_sem,
    recv_sem,
):
    nx, nz, nk = grid
    blocks = nx * nz * 2
    pm = lax.axis_index("pm")
    ka = lax.axis_index("ka")
    side = lax.axis_index("isdf")
    core = ka % 2
    z = (ka // 2) % nz
    x = ka // (2 * nz)
    nv, nc = xbuf.shape[2], xbuf.shape[3]
    nmu = cond.shape[3]
    nnu = vals.shape[4]
    half = nc // 2

    mate = ka + 1 - 2 * core
    above = (ka + REACH) % blocks
    below = (ka + blocks - REACH) % blocks
    across = blocks - 1 - ka

    def ka_of(x_at, z_at, core_at):
        return (x_at * nz + z_at) * 2 + core_at

    a_size = 4 * nx
    a_index = (x * 2 + core) * 2 + side

    def a_peer(step):
        other = (a_index + step) % a_size
        return {"ka": ka_of(other // 4, z, (other // 2) % 2), "isdf": other % 2}

    def b_peer(step):
        return {"ka": ka_of(x, (z + step) % nz, core)}

    here = {"pm": pm, "ka": ka, "isdf": side}

    def device(**change):
        return {**here, **change}

    counter = {"local": 0, "send": 0, "recv": 0}

    def take(kind, count=1):
        first = counter[kind]
        counter[kind] += count
        return first

    def local(src, dst):
        return pltpu.make_async_copy(src, dst, local_sem.at[take("local")])

    pending = []

    def remote(src, dst, recv, target):
        copy = pltpu.make_async_remote_copy(
            src_ref=src,
            dst_ref=dst,
            send_sem=send_sem.at[take("send")],
            recv_sem=recv_sem.at[recv],
            device_id=target,
            device_id_type=MESH,
        )
        return copy

    def launch(src, dst, recv, target):
        copy = remote(src, dst, recv, target)
        copy.start()
        pending.append(copy)

    def arrive(dst, recv):
        pltpu.make_async_remote_copy(
            src_ref=dst,
            dst_ref=dst,
            send_sem=send_sem.at[0],
            recv_sem=recv_sem.at[recv],
            device_id=device(isdf=1 - side),
            device_id_type=MESH,
        ).wait_recv()

    greeted = [
        device(pm=1 - pm),
        device(pm=0, ka=across),
        device(pm=1, ka=across),
        device(ka=above),
        device(ka=below),
    ]
    greeted += [device(**a_peer(step)) for step in range(1, a_size)]
    greeted += [device(**b_peer(step)) for step in range(1, nz)]
    barrier = pltpu.get_barrier_semaphore()
    for target in greeted:
        pl.semaphore_signal(barrier, inc=1, device_id=target, device_id_type=MESH)

    load_v = local(val_hbm, vals.at[REACH])
    load_c = local(cond_hbm, cond)
    load_x = local(amps.at[0, 0], xbuf)
    load_s = local(screened_hbm, screened)
    load_k = local(coulomb_hbm, coulomb)
    load_e = local(energy_hbm, energy)
    load_v.start()
    load_c.start()

    @pl.when(pm == 0)
    def _():
        load_x.start()

    load_s.start()
    load_k.start()
    load_e.start()
    pl.semaphore_wait(barrier, len(greeted))

    x_recv = take("recv")
    hop_recv = take("recv", 2)
    y_recv = take("recv", 2)
    y_pass_recv = take("recv", 2)
    v_recv = take("recv", SLOTS)
    g_recv = [take("recv", SLOTS) for _ in range(1 + KDEV)]
    send_x = remote(amps.at[0, 1], xbuf, x_recv, device(pm=1))
    send_hop = [remote(amps.at[0, 0, part, side], yhop.at[part], hop_recv + part, device(pm=0)) for part in range(2)]
    send_y = [
        remote(amps.at[0, 1, part, side], ybuf.at[part, side], y_recv + part, device(ka=across))
        for part in range(2)
    ]
    pass_y = [remote(yhop.at[part], ybuf.at[part, side], y_recv + part, device(ka=across)) for part in range(2)]

    @pl.when(pm == 1)
    def _():
        for copy in send_hop + send_y:
            copy.start()

    @pl.when(pm == 0)
    def _():
        send_x.start()

    mate_there = 1 + 2 * core
    mate_here = 3 - 2 * core
    pass_from = 4 - 4 * core
    pass_there = 3 - 2 * core
    passed_here = 1 + 2 * core
    direct_here = 4 * core

    def spread_block(block, landing, recv):
        launch(block, landing.at[0], recv, device(ka=above))
        launch(block, landing.at[SLOTS - 1], recv + SLOTS - 1, device(ka=below))
        launch(block, landing.at[mate_there], recv + mate_there, device(ka=mate))

    def pass_block(landing, recv):
        arrive(landing.at[pass_from], recv + pass_from)
        launch(landing.at[pass_from], landing.at[pass_there], recv + pass_there, device(ka=mate))

    my_mu = pl.ds(pl.multiple_of(side * nmu, nmu), nmu)
    my_half = pl.ds(pl.multiple_of(side * half, half), half)

    def transform(channel, k, z_real, z_imag, sign):
        stack = jnp.concatenate([z_real, z_imag], axis=0)
        with_real = dot_nn(stack, cond[0, k])
        with_imag = dot_nn(stack, cond[1, k])
        g_real = with_real[:nv] - sign * with_imag[nv:]
        g_imag = with_imag[:nv] + sign * with_real[nv:]
        g_all = jnp.concatenate([g_real, g_imag], axis=0)
        gbuf[channel, REACH, k] = jnp.transpose(g_all).astype(BF16)
        v_real = vals[REACH, 0, k, :, my_mu].astype(F32)
        v_imag = vals[REACH, 1, k, :, my_mu].astype(F32)
        rho_real = jnp.sum(v_real * g_real + v_imag * g_imag, axis=0, keepdims=True)
        rho_imag = jnp.sum(v_real * g_imag - v_imag * g_real, axis=0, keepdims=True)
        return rho_real, rho_imag

    def pairs(channel, slot):
        def one(k, carry):
            v_real = vals[slot, 0, k]
            v_imag = vals[slot, 1, k]
            coef = gbuf[channel, slot, k]
            at = slot * KDEV + k
            mbuf[at, 0] = dot_nn(coef, jnp.concatenate([v_real, v_imag], axis=0)).astype(BF16)
            mbuf[at, 1] = dot_nn(coef, jnp.concatenate([-v_imag, v_real], axis=0)).astype(BF16)
            return carry

        lax.fori_loop(0, KDEV, one, 0)

    load_c.wait()
    load_v.wait()

    @pl.when(pm == 0)
    def _():
        load_x.wait()

    @pl.when(pm == 1)
    def _():
        arrive(xbuf, x_recv)

    rho_x = [transform(0, k, xbuf[0, k], xbuf[1, k], 1.0) for k in range(KDEV)]

    @pl.when(pm == 0)
    def _():
        for part in range(2):
            arrive(yhop.at[part], hop_recv + part)
            pass_y[part].start()

    spread_block(val_hbm, vals, v_recv)
    spread_block(gbuf.at[0, REACH], gbuf.at[0], g_recv[0])
    forwards = [
        remote(ybuf.at[part, side], ybuf.at[part, side], y_pass_recv + part, device(isdf=1 - side))
        for part in range(2)
    ]
    pending.extend(forwards)

    def forward_y():
        for part in range(2):
            arrive(ybuf.at[part, side], y_recv + part)
            forwards[part].start()

    @pl.when(pm == 1)
    def _():
        forward_y()


    def wait_slot(landing, recv, slot):
        arrive(landing.at[slot], recv + slot)

    def screen(k, slots, fresh):
        rows = 16
        terms = []
        for slot in slots:
            for visitor in range(KDEV):
                at = slot * KDEV + visitor
                terms.append((at, classes[0, (ka * KDEV + nk - (SLOTS - 1) - k + at) % nk]))

        def one(i, carry):
            row = pl.ds(pl.multiple_of(i * rows, rows), rows)
            for column in range(0, nnu, 128):
                col = pl.ds(column, 128)
                straight = None if fresh else sbuf[k, 0, row, col]
                turned = None if fresh else sbuf[k, 1, row, col]
                crossed = None
                for at, kind in terms:
                    w_real, w_imag = screened[kind, 0, row, col], screened[kind, 1, row, col]
                    m_real, m_imag = mbuf[at, 0, row, col], mbuf[at, 1, row, col]
                    first, second = w_real * m_real, w_imag * m_imag
                    mixed = w_real * m_imag + w_imag * m_real
                    straight = first if straight is None else straight + first
                    crossed = second if crossed is None else crossed + second
                    turned = mixed if turned is None else turned + mixed
                sbuf[k, 0, row, col] = straight - crossed
                sbuf[k, 1, row, col] = turned
            return carry

        lax.fori_loop(0, nmu // rows, one, 0)

    late = (pass_from, direct_here, passed_here)

    def gather(channel, slots):
        flows = [(gbuf.at[1, :, k], g_recv[1 + k]) for k in range(KDEV)]
        if channel == 0:
            flows = [(vals, v_recv), (gbuf.at[0], g_recv[0])]
        for slot in slots:
            for landing, recv in flows:
                if slot is pass_from:
                    pass_block(landing, recv)
                else:
                    wait_slot(landing, recv, slot)
            pairs(channel, slot)

    pairs(0, REACH)
    load_k.wait()
    coulomb_high[...] = coulomb[...].astype(BF16)
    coulomb_low[...] = (coulomb[...] - coulomb[...].astype(BF16).astype(F32)).astype(BF16)
    gather(0, (mate_here,))
    load_s.wait()
    for k in range(KDEV):
        screen(k, (REACH, mate_here), True)

    @pl.when(pm == 0)
    def _():
        forward_y()

    for part in range(2):
        arrive(ybuf.at[part, 1 - side], y_pass_recv + part)
    mirrored = [lax.rem(mirror[k], KDEV) for k in range(KDEV)]
    rho_y = []
    for k in range(KDEV):
        rho_y.append(transform(1, k, ybuf[0, mirrored[k]], ybuf[1, mirrored[k]], -1.0))
        spread_block(gbuf.at[1, REACH, k], gbuf.at[1, :, k], g_recv[1 + k])

    density = jnp.concatenate(
        [
            sum(part[0] for part in rho_x + rho_y),
            sum(part[1] for part in rho_x + rho_y),
            jnp.zeros((6, nmu), F32),
        ],
        axis=0,
    )
    rest = density - density.astype(BF16).astype(F32)
    both = dot_nt(jnp.concatenate([density, rest], axis=0).astype(BF16), coulomb_high[...])
    share = both[:8] + both[8:] + dot_nt(density.astype(BF16), coulomb_low[...])
    lanes = 128
    pieces = nmu // lanes
    for there in range(2):
        for part in range(2):
            for piece in range(pieces):
                column = there * nmu + piece * lanes
                row = part * pieces + piece
                ar_out[there, pl.ds(row, 1), :] = share[part : part + 1, column : column + lanes]
    a_at = take("recv", a_size)
    for step in range(1, a_size):
        peer = a_peer(step)
        launch(ar_out.at[peer["isdf"]], ar_a.at[a_index], a_at + a_index, device(**peer))
    ar_a[a_index] = ar_out[side]
    b_at = take("recv", nz)

    def second_stage():
        for step in range(1, a_size):
            other = (a_index + step) % a_size
            arrive(ar_a.at[other], a_at + other)
        ar_b[z] = jnp.sum(ar_a[...], axis=0)
        for step in range(1, nz):
            launch(ar_b.at[z], ar_b.at[z], b_at + z, device(**b_peer(step)))

    def last_stage():
        for step in range(1, nz):
            other = (z + step) % nz
            arrive(ar_b.at[other], b_at + other)
        total = 2.0 * jnp.sum(ar_b[...], axis=0)
        return [
            jnp.concatenate([total[part * pieces + i : part * pieces + i + 1] for i in range(pieces)], axis=1)
            for part in range(2)
        ]

    def back(channel, k):
        v_real, v_imag = vals[REACH, 0, k], vals[REACH, 1, k]
        summed = dot_nt(sbuf[k, 0], jnp.concatenate([v_real, v_imag], axis=0))
        summed = summed + dot_nt(sbuf[k, 1], jnp.concatenate([-v_imag, v_real], axis=0))
        backs[channel, k] = jnp.transpose(summed)

    gather(0, late)
    screen(0, late, False)
    back(0, 0)
    second_stage()
    screen(1, late, False)
    back(0, 1)

    rs_at = take("recv", 2 * KDEV)
    land_x_at = take("recv", KDEV)
    cross_at = take("recv", 2 * KDEV)
    back_x = []

    def produce(channel, k, u_real, u_imag):
        v_real = vals[REACH, 0, k, :, my_mu].astype(F32)
        v_imag = vals[REACH, 1, k, :, my_mu].astype(F32)
        exchange = jnp.concatenate([u_real * v_real - u_imag * v_imag, u_real * v_imag + u_imag * v_real], axis=0)
        field = (exchange - backs[channel, k]).astype(BF16)
        with_real = dot_nt(field, cond[0, k])
        with_imag = dot_nt(field, cond[1, k])
        for part, value in (
            (0, with_real[:nv] + with_imag[nv:]),
            (1, with_real[nv:] - with_imag[:nv]),
        ):
            owns[channel, k, part] = jnp.where(side == 0, value[:, :half], value[:, half:])
            rs_send[channel, k, part] = jnp.where(side == 0, value[:, half:], value[:, :half]).astype(BF16)
        at = channel * KDEV + k
        launch(rs_send.at[channel, k], rs_recv.at[channel, k], rs_at + at, device(isdf=1 - side))

    def complete(channel, k):
        arrive(rs_recv.at[channel, k], rs_at + channel * KDEV + k)
        for part in range(2):
            if channel == 0:
                amp = xbuf[part, k, :, my_half].astype(F32)
            else:
                amp = ybuf[part, mirrored[k], :, my_half].astype(F32)
                amp = -amp if part == 1 else amp
            value = energy[k] * amp + owns[channel, k, part] + rs_recv[channel, k, part].astype(F32)
            if channel == 1 and part == 1:
                value = -value
            results[channel, k, part] = value.astype(BF16)
        if channel == 1:
            launch(results.at[1, k], land_y.at[pm, k], cross_at + pm * KDEV + k, device(pm=1, ka=across))
        else:
            copy = remote(results.at[0, k], land_x.at[k], land_x_at + k, device(pm=0))
            back_x.append(copy)

            @pl.when(pm == 1)
            def _():
                copy.start()

    pairs(1, REACH)
    gather(1, (mate_here,))
    for k in range(KDEV):
        screen(k, (REACH, mate_here), True)
    gather(1, late)
    screen(0, late, False)
    back(1, 0)
    u_real, u_imag = last_stage()
    produce(1, 0, u_real, u_imag)
    screen(1, late, False)
    back(1, 1)
    produce(1, 1, u_real, u_imag)
    load_e.wait()
    complete(1, 0)
    produce(0, 0, u_real, u_imag)
    produce(0, 1, u_real, u_imag)
    complete(1, 1)
    complete(0, 0)
    complete(0, 1)

    @pl.when(pm == 0)
    def _():
        for k in range(KDEV):
            out[0, 0, :, k] = results[0, k]
        for k in range(KDEV):
            arrive(land_x.at[k], land_x_at + k)
            out[0, 1, :, k] = land_x[k]

    @pl.when(pm == 1)
    def _():
        for b in range(2):
            for k in range(KDEV):
                arrive(land_y.at[b, k], cross_at + b * KDEV + k)
        for b in range(2):
            for k in range(KDEV):
                out[0, b, :, k] = land_y[b, mirrored[k]]

    for copy in pending:
        copy.wait_send()

    @pl.when(pm == 0)
    def _():
        for copy in [send_x] + pass_y:
            copy.wait_send()

    @pl.when(pm == 1)
    def _():
        for copy in send_hop + send_y + back_x:
            copy.wait_send()


def per_device(grid, amplitudes, conduction, valence, energy, screened, coulomb, mirror, transfer_class):
    nx, nz = grid[:2]
    _, vectors, _, _, nv, nc = amplitudes.shape
    nmu = conduction.shape[3]
    nnu = valence.shape[3]
    half = energy.shape[2]
    pair = (2, KDEV)
    hbm = pl.BlockSpec(memory_space=pl.ANY)
    smem = pl.BlockSpec(memory_space=pltpu.SMEM)
    vmem = pl.BlockSpec(memory_space=pltpu.VMEM)
    return pl.pallas_call(
        functools.partial(kernel, grid),
        out_shape=jax.ShapeDtypeStruct((1, vectors, 2, KDEV, nv, half), BF16),
        in_specs=[hbm] * 6 + [smem] * 2,
        out_specs=vmem,
        scratch_shapes=[
            pltpu.VMEM(conduction.shape, BF16),
            pltpu.VMEM((SLOTS,) + valence.shape, BF16),
            pltpu.VMEM(energy.shape, F32),
            pltpu.VMEM(screened.shape, BF16),
            pltpu.VMEM(coulomb.shape, F32),
            pltpu.VMEM((2, KDEV, nv, nc), BF16),
            pltpu.VMEM((2, KDEV, nv, nc), BF16),
            pltpu.VMEM((2, nv, nc), BF16),
            pltpu.VMEM((2, SLOTS, KDEV, nmu, 2 * nv), BF16),
            pltpu.VMEM((SLOTS * KDEV, 2, nmu, nnu), BF16),
            pltpu.VMEM((KDEV, 2, nmu, nnu), BF16),
            pltpu.VMEM((2, KDEV, 2 * nv, nmu), F32),
            pltpu.VMEM((2, KDEV, 2, nv, half), F32),
            pltpu.VMEM((2, KDEV, 2, nv, half), BF16),
            pltpu.VMEM((2, KDEV, 2, nv, half), BF16),
            pltpu.VMEM((2, KDEV, 2, nv, half), BF16),
            pltpu.VMEM((KDEV, 2, nv, half), BF16),
            pltpu.VMEM((2, KDEV, 2, nv, half), BF16),
            pltpu.VMEM(coulomb.shape, BF16),
            pltpu.VMEM(coulomb.shape, BF16),
            pltpu.VMEM((2, 2 * nmu // 128, 128), F32),
            pltpu.VMEM((4 * nx, 2 * nmu // 128, 128), F32),
            pltpu.VMEM((nz, 2 * nmu // 128, 128), F32),
            pltpu.SemaphoreType.DMA((6,)),
            pltpu.SemaphoreType.DMA((80,)),
            pltpu.SemaphoreType.DMA((80,)),
        ],
        compiler_params=pltpu.CompilerParams(
            collective_id=0, has_side_effects=True, vmem_limit_bytes=60 * 2**20
        ),
    )(amplitudes, conduction, valence, energy, screened, coulomb, mirror, transfer_class)


def solution(mesh):
    blocks = mesh.shape["ka"]
    nz = 16 if blocks >= 128 else blocks // 4
    nx = blocks // (2 * nz)
    return jax.shard_map(
        functools.partial(per_device, (nx, nz, KDEV * blocks)),
        mesh=mesh,
        in_specs=(
            P("pm", None, None, "ka", None, None),
            P(None, "ka", None, "isdf"),
            P(None, "ka", None, None),
            P("ka", None, "isdf"),
            P(None, None, "isdf", None),
            P(None, "isdf"),
            P("ka"),
            P("ka", None),
        ),
        out_specs=P("pm", None, None, "ka", None, "isdf"),
        check_vma=False,
    )
```
